256 devices in a mesh: expert: 64 (over x_hi, y, z), dp: 4 (over x_lo, core).
Axes of the slice: x: 4 (x_hi: 2, x_lo: 2; x = x_hi * 2 + x_lo), y: 4, z: 8, core: 2. Of those that a mesh axis runs over, the one named last changes fastest.
Arguments:
- tokens: bfloat16 [8192, 2048], P(('expert', 'dp')), may hold values from -6 to 6
- cotangent: bfloat16 [8192, 2048], P(('expert', 'dp')), may hold values from -6 to 6
- routes: int32 [8192, 8], P(('expert', 'dp')), may hold values from 0 to 63, all different within a row; in each aligned block of 32 rows (0 to 31, 32 to 63, ...) at most 6 rows name the same one
- route_weights: float32 [8192, 8], P(('expert', 'dp')), may hold values from 0.05 to 0.25
- matching: int32 [64], replicated, may hold values from 0 to 63, as said below
- gate_up: bfloat16 [64, 2, 768, 2048], P('expert', None, 'dp'), may hold values from -0.125 to 0.125
- down: bfloat16 [64, 768, 2048], P('expert', 'dp'), may hold values from -0.21875 to 0.21875
- gate_up_m: bfloat16 [64, 2, 768, 2048], P('expert', None, 'dp'), may hold values from -3 to 3
- gate_up_v: bfloat16 [64, 2, 768, 2048], P('expert', None, 'dp'), may hold values from 0.0099487305 to 1
- down_m: bfloat16 [64, 768, 2048], P('expert', 'dp'), may hold values from -3 to 3
- down_v: bfloat16 [64, 768, 2048], P('expert', 'dp'), may hold values from 0.0099487305 to 1
Outputs:
- layer_out: bfloat16 [8192, 2048], P(('expert', 'dp'))
- input_grad: bfloat16 [8192, 2048], P(('expert', 'dp'))
- new_gate_up: bfloat16 [64, 2, 768, 2048], P('expert', None, 'dp')
- new_down: bfloat16 [64, 768, 2048], P('expert', 'dp')
The draws below stay inside these ranges and needn't reach their ends.
Inputs may be any that keep to these rules, and one draw needn't show every extreme that they name: matching[i] is either i or the index that differs from i in its highest bit (32 away); matching[matching[i]] = i, and exactly 16 pairs are exchanged, among them always the pair of index 0 and the pair of index 31. `routes`: within the 32 rows of one device, each expert is named at most 6 times, and this bound is reached.
All inputs are finite; a program needn't handle non-finite values.
Results may differ from the reference program's by a relative error of at most 0.0075.
Values may be sent and summed in bfloat16 or wider, within the bound.
No kernel may reach another device: no remote copies, remote signals or barrier semaphores. Data moves between devices by JAX's collectives and lax.ppermute only.
A program may use at most 128 MiB of HBM per device.

```python
import math
import jax
import jax.numpy as jnp
import numpy as np
from jax import lax

D = 2048
FF = 768
TOP = 8
TOK_DEV = 32
EXPERTS = 64
PAIRS = 16
CAP = 6
TOKENS = 8192
N_EXPERT = 64
N_DP = 4


def draw_matching(key, part):
    key = jax.random.fold_in(key, 7)
    half_count = EXPERTS // 2
    ranking = jax.random.permutation(key, half_count - 2)
    middle = ranking < PAIRS - 2
    chosen = jnp.concatenate([jnp.ones((1,), bool), middle, jnp.ones((1,), bool)])
    lower = jnp.arange(half_count, dtype=jnp.int32)
    partner_low = jnp.where(chosen, lower + half_count, lower)
    partner_high = jnp.where(chosen, lower, lower + half_count)
    return jnp.concatenate([partner_low, partner_high]).astype(jnp.int32)


def block_scale(key, extent, cuts, low, largest):
    factor_of, own = 1.0, jax.random.fold_in(key, 6)
    for position, parts in cuts:
        draws = jnp.exp(jax.random.uniform(jax.random.fold_in(own, position), (parts,), jnp.float32, low / len(cuts), largest / len(cuts)))
        factor_of = factor_of * jnp.repeat(draws, extent[position] // parts).reshape([-1 if axis == position else 1 for axis in range(len(extent))])
    return factor_of


def deal_out(rng, own, number, rows, count, top, most, lean):
    order = jax.random.permutation(rng, count)
    crowded, ordinary = load_shares(count, rows * top, most, lean, True), load_shares(count, rows * top, most, lean, False)
    places = jnp.arange(count)

    def named(lengths, turn):
        used = int((lengths > 0).sum())
        fixed = max(1, used // 4)
        shifted = fixed + (places - fixed + turn * (used - fixed)) % max(1, count - fixed)
        return jnp.zeros((count,), jnp.int32).at[order[jnp.where(places < fixed, places, shifted)]].set(jnp.asarray(lengths, jnp.int32))

    lengths = jnp.where(number % 4 == 0, named(crowded, number // 4), named(ordinary, number - number // 4 - 1))
    mixed = jax.random.permutation(jax.random.fold_in(own, 3), count)
    source_of, sink = mixed[0:count // 2 * 2:2], mixed[1:count // 2 * 2:2]
    slack = jnp.minimum(lengths[source_of] - 1, most - lengths[sink]) // 2
    slack = jnp.where((source_of == order[0]) | (sink == order[0]) | (lengths[sink] == 0), 0, jnp.maximum(slack, 0))
    shifted = jax.random.randint(jax.random.fold_in(own, 4), (count // 2,), 0, 1 << 20) % (slack + 1)
    lengths = lengths.at[source_of].add(-shifted).at[sink].add(shifted)
    members = jnp.searchsorted(jnp.cumsum(lengths), jnp.arange(rows * top), side="right").astype(jnp.int32)
    listing = members.reshape(top, rows).T
    listing = listing[jax.random.permutation(jax.random.fold_in(own, 1), rows)]
    turn = jax.random.randint(jax.random.fold_in(own, 2), (rows, 1), 0, top)
    return jnp.take_along_axis(listing, (jnp.arange(top)[None, :] + turn) % top, axis=1)


def load_shares(count, total, limit, slope, full):
    portions = [(1 << 20) // math.isqrt(standing ** slope) + 1 for standing in range(1, count + 1)]
    largest = limit if full else min(limit, max(-(-total // count), total * portions[0] // sum(portions)))
    least = 1 if total - largest >= count - 1 else 0
    given, rest = [largest] + [least] * (count - 1), total - largest - least * (count - 1)
    while rest > 0:
        candidates = [i for i in range(1, count) if given[i] < largest] or [i for i in range(1, count) if given[i] < limit]
        mass, remaining = sum([portions[i] for i in candidates]), rest
        for i in candidates:
            extra = min(limit - given[i], max(1, remaining * portions[i] // mass), rest)
            given[i] = given[i] + extra
            rest = rest - extra
    return np.array(given)


def scatter_about(rng, dims, spread, most, split=(), held_as=jnp.bfloat16):
    drawn = jax.random.normal(rng, dims, jnp.float32) * spread
    if len(split) > 0:
        drawn = block_scale(rng, dims, split, -0.22, 0.18) * drawn
    return jnp.clip(drawn, min=-most, max=most).astype(held_as)


def setup_inputs(seed: int = 0) -> dict:
    seeds = jax.random.split(jax.random.key(seed), 12)
    tokens = scatter_about(seeds[0], (TOKENS, D), 1.0, 6.0, ((0, 256),))
    cotangent = scatter_about(seeds[1], (TOKENS, D), 1.0, 6.0, ((0, 256),))
    routes_keys = jax.random.split(jax.random.fold_in(seeds[2], 1), TOKENS // TOK_DEV)
    routes_turns = jax.random.permutation(jax.random.fold_in(seeds[2], 3), TOKENS // TOK_DEV)
    routes = jax.vmap(lambda own, number: deal_out(jax.random.fold_in(seeds[2], 2), own, number, TOK_DEV, EXPERTS, TOP, CAP, 2))(routes_keys, routes_turns).reshape((TOKENS, TOP))
    route_weights = jnp.clip(0.05 + 0.2 * jax.random.uniform(seeds[3], (TOKENS, TOP), jnp.float32) ** block_scale(seeds[3], (TOKENS, TOP), ((0, 256),), -0.2, 0.2), 0.05, 0.25)
    matching = draw_matching(jax.random.fold_in(seeds[11], 71), 0)
    gate_up = scatter_about(seeds[5], (EXPERTS, 2, FF, D), D ** -0.5, 0.125, ((0, 64), (2, 4)))
    down = scatter_about(seeds[6], (EXPERTS, FF, D), FF ** -0.5, 0.21875, ((0, 64), (1, 4)))
    gate_up_m = scatter_about(seeds[7], (EXPERTS, 2, FF, D), 0.5, 3.0, ((0, 64), (2, 4)))
    gate_up_v = jnp.clip(jnp.exp(math.log(1.0) - 4.61031033 * jax.random.uniform(seeds[8], (EXPERTS, 2, FF, D), jnp.float32) ** block_scale(seeds[8], (EXPERTS, 2, FF, D), ((0, 64), (2, 4)), -0.2, 0.2)), 0.0099487305, 1.0).astype(jnp.bfloat16)
    down_m = scatter_about(seeds[9], (EXPERTS, FF, D), 0.5, 3.0, ((0, 64), (1, 4)))
    down_v = jnp.clip(jnp.exp(math.log(1.0) - 4.61031033 * jax.random.uniform(seeds[10], (EXPERTS, FF, D), jnp.float32) ** block_scale(seeds[10], (EXPERTS, FF, D), ((0, 64), (1, 4)), -0.2, 0.2)), 0.0099487305, 1.0).astype(jnp.bfloat16)
    return dict(tokens=tokens, cotangent=cotangent, routes=routes, route_weights=route_weights, matching=matching, gate_up=gate_up, down=down, gate_up_m=gate_up_m, gate_up_v=gate_up_v, down_m=down_m, down_v=down_v)


BETA_ONE = 0.9
BETA_TWO = 0.95
STEP_RATE = 0.01
ADAM_EPS = 1e-08

def adam_update(weight, moment_one, moment_two, gradient):
    one_new = BETA_ONE * moment_one.astype(jnp.float32) + (1.0 - BETA_ONE) * gradient
    two_new = BETA_TWO * moment_two.astype(jnp.float32) + (1.0 - BETA_TWO) * gradient * gradient
    return (weight.astype(jnp.float32) - STEP_RATE * one_new / (jnp.sqrt(two_new) + ADAM_EPS)).astype(jnp.bfloat16)

def rounded(value):
    return lax.optimization_barrier(value.astype(jnp.bfloat16)).astype(jnp.float32)

def contract_last(left, right):
    return lax.dot_general(left, right, (((1,), (1,)), ((), ())), preferred_element_type=jnp.float32)

def contract_first(left, right):
    return lax.dot_general(left, right, (((0,), (0,)), ((), ())), preferred_element_type=jnp.float32)

def reference(tokens, cotangent, routes, route_weights, matching, gate_up, down, gate_up_m, gate_up_v, down_m, down_v):
    top_count = routes.shape[1]
    groups = EXPERTS * N_DP
    group_most = N_EXPERT * CAP
    flat_expert = routes.reshape(-1).astype(jnp.int32)
    flat_token = jnp.repeat(jnp.arange(TOKENS, dtype=jnp.int32), top_count)
    flat_weight = route_weights.reshape(-1)
    flat_replica = flat_token // TOK_DEV % N_DP
    group_id = flat_expert * N_DP + flat_replica
    sort_order = jnp.argsort(group_id, stable=True).astype(jnp.int32)
    counts = jnp.bincount(group_id, length=groups).astype(jnp.int32)
    starts = (jnp.cumsum(counts) - counts).astype(jnp.int32)
    padded = jnp.concatenate([sort_order, jnp.zeros((group_most,), jnp.int32)])
    lane_ids = jnp.arange(group_most, dtype=jnp.int32)

    def one_expert(running_sums, expert):
        out_sum, grad_sum = running_sums
        w_gate = gate_up[expert, 0]
        w_up = gate_up[expert, 1]
        w_down = down[expert]
        total_gate = jnp.zeros((FF, D), jnp.float32)
        total_up = jnp.zeros((FF, D), jnp.float32)
        total_down = jnp.zeros((FF, D), jnp.float32)
        for replica in range(N_DP):
            slot_group = expert * N_DP + replica
            picked = lax.dynamic_slice(padded, (starts[slot_group],), (group_most,))
            live_rows = lane_ids < counts[slot_group]
            token_ids = flat_token[picked]
            weight = jnp.where(live_rows, flat_weight[picked], 0.0)
            rows_x = jnp.where(live_rows[:, None], tokens[token_ids], 0).astype(jnp.bfloat16)
            rows_d = (weight[:, None] * cotangent[token_ids].astype(jnp.float32)).astype(jnp.bfloat16)
            pre_gate = contract_last(rows_x, w_gate)
            pre_up = contract_last(rows_x, w_up)
            gate_sig = jax.nn.sigmoid(pre_gate)
            hidden = (pre_gate * gate_sig * pre_up).astype(jnp.bfloat16)
            out_rows = jnp.dot(hidden, w_down, preferred_element_type=jnp.float32).astype(jnp.bfloat16)
            d_hidden = contract_last(rows_d, w_down)
            d_gate = (d_hidden * pre_up * gate_sig * (1.0 + pre_gate * (1.0 - gate_sig))).astype(jnp.bfloat16)
            d_up = (d_hidden * pre_gate * gate_sig).astype(jnp.bfloat16)
            d_rows = (jnp.dot(d_gate, w_gate, preferred_element_type=jnp.float32) + jnp.dot(d_up, w_up, preferred_element_type=jnp.float32)).astype(jnp.bfloat16)
            out_sum = out_sum.at[token_ids].add(weight[:, None] * out_rows.astype(jnp.float32))
            grad_sum = grad_sum.at[token_ids].add(d_rows.astype(jnp.float32))
            total_gate = total_gate + rounded(contract_first(d_gate, rows_x))
            total_up = total_up + rounded(contract_first(d_up, rows_x))
            total_down = total_down + rounded(contract_first(hidden, rows_d))
        grad_gu = jnp.stack([total_gate, total_up])
        new_gu = adam_update(gate_up[expert], gate_up_m[expert], gate_up_v[expert], grad_gu)
        new_dn = adam_update(down[expert], down_m[expert], down_v[expert], total_down)
        return ((out_sum, grad_sum), (new_gu, new_dn))
    initial = (jnp.zeros((TOKENS, D), jnp.float32), jnp.zeros((TOKENS, D), jnp.float32))
    (out_sum, grad_sum), (all_gu, all_down) = lax.scan(one_expert, initial, jnp.arange(EXPERTS, dtype=jnp.int32))
    new_gate_up = jnp.take(all_gu, matching, axis=0)
    new_down = jnp.take(all_down, matching, axis=0)
    return (out_sum.astype(jnp.bfloat16), grad_sum.astype(jnp.bfloat16), new_gate_up, new_down)
```

```python
import jax
import jax.numpy as jnp
from jax import lax
from jax.experimental import pallas as pl
from jax.experimental.pallas import tpu as pltpu
from jax.sharding import Mesh, PartitionSpec as P

BETA_ONE = 0.9
BETA_TWO = 0.95
STEP_RATE = 0.01
ADAM_EPS = 1e-08

F32 = jnp.float32
BF16 = jnp.bfloat16
CAP = 6
RINGS = ("y", "z")
ALL = ("xh", "y", "z", "xl", "core")


def swap(block, axis):
    return lax.ppermute(block, axis, [(0, 1), (1, 0)])


def after(value, *earlier):
    return lax.optimization_barrier((value, *earlier))[0]


def adam_update(weight, moment_one, moment_two, gradient):
    one_new = BETA_ONE * moment_one.astype(F32) + (1.0 - BETA_ONE) * gradient
    two_new = BETA_TWO * moment_two.astype(F32) + (1.0 - BETA_TWO) * gradient * gradient
    return (weight.astype(F32) - STEP_RATE * one_new / (jnp.sqrt(two_new) + ADAM_EPS)).astype(BF16)


def dot_nt(left, right):
    return lax.dot_general(left, right, (((1,), (1,)), ((), ())), preferred_element_type=F32)


def dot_nn(left, right):
    return lax.dot_general(left, right, (((1,), (0,)), ((), ())), preferred_element_type=F32)


def dot_tn(left, right):
    return lax.dot_general(left, right, (((0,), (0,)), ((), ())), preferred_element_type=F32)


CHUNK = 256


def expert_kernel(x_ref, d_ref, w_own, w_xl, w_pair, o_ref, dx_ref, g_own, g_xl, g_pair,
                  w_all, g_all, o_acc, dx_acc, in_sem, out_sem):
    share = w_own.shape[1]
    sources = (w_own, w_xl, w_pair.at[0], w_pair.at[1])
    targets = (g_own, g_xl, g_pair.at[0], g_pair.at[1])
    loads = [
        pltpu.make_async_copy(src, w_all.at[:, pl.ds(i * share, share)], in_sem.at[i])
        for i, src in enumerate(sources)
    ]
    stores = [
        pltpu.make_async_copy(g_all.at[:, pl.ds(i * share, share)], dst, out_sem.at[i])
        for i, dst in enumerate(targets)
    ]
    for load in loads:
        load.start()
    for load in loads:
        load.wait()
    chunks = w_all.shape[1] // CHUNK

    def step(c, carry):
        rows = pl.ds(pl.multiple_of(c * CHUNK, CHUNK), CHUNK)
        x = x_ref[...]
        d = d_ref[...]
        a = dot_nt(x, w_all[0, rows, :])
        u = dot_nt(x, w_all[1, rows, :])
        s = 1.0 / (1.0 + jnp.exp(-a))
        h = (a * s * u).astype(BF16)
        dh = dot_nt(d, w_all[2, rows, :])
        da = (dh * u * s * (1.0 + a * (1.0 - s))).astype(BF16)
        du = (dh * a * s).astype(BF16)
        o = dot_nn(h, w_all[2, rows, :])
        dx = dot_nn(da, w_all[0, rows, :]) + dot_nn(du, w_all[1, rows, :])

        @pl.when(c == 0)
        def _():
            o_acc[...] = o
            dx_acc[...] = dx

        @pl.when(c > 0)
        def _():
            o_acc[...] += o
            dx_acc[...] += dx

        g_all[0, rows, :] = dot_tn(da, x).astype(BF16)
        g_all[1, rows, :] = dot_tn(du, x).astype(BF16)
        g_all[2, rows, :] = dot_tn(h, d).astype(BF16)
        return carry

    lax.fori_loop(0, chunks, step, 0)
    for store in stores:
        store.start()
    o_ref[...] = o_acc[...].astype(BF16)
    dx_ref[...] = dx_acc[...].astype(BF16)
    for store in stores:
        store.wait()


def expert_step(x, d, w_own, w_xl, w_pair):
    rows, feature = x.shape
    share = w_own.shape[1]
    any_spec = pl.BlockSpec(memory_space=pl.ANY)
    vmem_spec = pl.BlockSpec(memory_space=pltpu.VMEM)
    row_shape = jax.ShapeDtypeStruct((rows, feature), BF16)
    part_shape = jax.ShapeDtypeStruct(w_own.shape, BF16)
    pair_shape = jax.ShapeDtypeStruct(w_pair.shape, BF16)
    return pl.pallas_call(
        expert_kernel,
        out_shape=(row_shape, row_shape, part_shape, part_shape, pair_shape),
        in_specs=[vmem_spec, vmem_spec, any_spec, any_spec, any_spec],
        out_specs=(vmem_spec, vmem_spec, any_spec, any_spec, any_spec),
        scratch_shapes=[
            pltpu.VMEM((3, 4 * share, feature), BF16),
            pltpu.VMEM((3, 4 * share, feature), BF16),
            pltpu.VMEM((rows, feature), F32),
            pltpu.VMEM((rows, feature), F32),
            pltpu.SemaphoreType.DMA((4,)),
            pltpu.SemaphoreType.DMA((4,)),
        ],
        compiler_params=pltpu.CompilerParams(vmem_limit_bytes=56 * 1024 * 1024),
        cost_estimate=pl.CostEstimate(
            flops=18 * rows * feature * 4 * share,
            bytes_accessed=2 * (4 * rows * feature + 24 * share * feature),
            transcendentals=rows * 4 * share,
        ),
    )(x, d, w_own, w_xl, w_pair)


def split_three(value):
    high = value.astype(BF16)
    rest = value - high.astype(F32)
    middle = rest.astype(BF16)
    low = (rest - middle.astype(F32)).astype(BF16)
    return high, middle, low


def body(tokens, cotangent, routes, route_weights, matching, gate_up, down, gate_up_m, gate_up_v,
         down_m, down_v):
    half = lax.axis_index("xh")
    rings = lax.axis_size("y") * lax.axis_size("z")
    self_index = half * rings + lax.axis_index("y") * lax.axis_size("z") + lax.axis_index("z")
    swapped = jnp.sum(jnp.where(jnp.arange(2 * rings) == self_index, matching, 0)) != self_index
    count, feature = tokens.shape
    slots = 2 * CAP

    packed = jnp.concatenate([tokens, cotangent])
    packed_other = swap(packed, "xh")
    routes_other = swap(routes, "xh")
    weights_other = swap(route_weights, "xh")
    source = jnp.concatenate([packed, packed_other])

    w_own = jnp.concatenate([gate_up[0], down])
    w_first = after(w_own, packed_other, routes_other, weights_other)
    w_xl = swap(w_first, "xl")
    w_pair = swap(jnp.stack([w_own, w_xl]), "core")

    both_routes = jnp.stack([routes, routes_other])
    both_weights = jnp.stack([route_weights, weights_other])
    ring_ids = jnp.arange(rings, dtype=jnp.int32)
    hit = both_routes[..., None] == half * rings + ring_ids
    used = jnp.any(hit, axis=2)
    scale = jnp.sum(jnp.where(hit, both_weights[..., None], 0.0), axis=2)
    earlier = jnp.cumsum(used.astype(jnp.int32), axis=1) - used
    slot = earlier + CAP * jnp.arange(2, dtype=jnp.int32)[:, None, None]
    slot = jnp.where(used, slot, -1)
    slot_ids = jnp.arange(slots, dtype=jnp.int32)
    select = jnp.transpose(slot, (2, 0, 1))[:, None] == slot_ids[None, :, None, None]
    row_scale = jnp.sum(jnp.where(select, jnp.transpose(scale, (2, 0, 1))[:, None], 0.0), axis=(2, 3))
    select_b = select.astype(BF16)
    none = jnp.zeros_like(select_b)
    pick_x = jnp.stack([select_b, none], axis=3)
    pick_c = jnp.stack([none, select_b], axis=3)
    pick = jnp.concatenate([pick_x, pick_c], axis=1).reshape(rings * 2 * slots, 4 * count)
    factor = jnp.concatenate([jnp.ones_like(row_scale), row_scale], axis=1).reshape(-1, 1)
    send = (dot_nn(pick, source) * factor).astype(BF16).reshape(rings, 2 * slots, feature)

    recv = lax.all_to_all(send, RINGS, split_axis=0, concat_axis=0, tiled=True)
    rows_x = recv[:, :slots].reshape(rings * slots, feature)
    rows_d = recv[:, slots:].reshape(rings * slots, feature)

    out_rows, dx_rows, g_own, g_xl, g_pair = expert_step(rows_x, rows_d, w_own, w_xl, w_pair)

    g_core = swap(g_pair, "core")
    back_send = jnp.concatenate(
        [out_rows.reshape(rings, slots, feature), dx_rows.reshape(rings, slots, feature)], axis=1
    )
    back = lax.all_to_all(back_send, RINGS, split_axis=0, concat_axis=0, tiled=True)
    moments_one = (gate_up_m[0, 0], gate_up_m[0, 1], down_m[0])
    moments_two = (gate_up_v[0, 0], gate_up_v[0, 1], down_v[0])
    updated = []
    for i in range(3):
        to_other = (g_xl[i].astype(F32) + g_core[1, i].astype(F32)).astype(BF16)
        gradient = g_own[i].astype(F32) + g_core[0, i].astype(F32) + swap(to_other, "xl").astype(F32)
        new = adam_update(w_own[i], moments_one[i], moments_two[i], gradient)
        updated.append(jnp.where(swapped, swap(new, "xh"), new))

    mix = jnp.transpose(select, (2, 3, 0, 1))
    mix_y = jnp.where(mix, row_scale, 0.0)
    mix_y = jnp.concatenate([mix_y, jnp.zeros_like(mix_y)], axis=3).reshape(2 * count, -1)
    mix_d = mix.astype(BF16)
    mix_d = jnp.concatenate([jnp.zeros_like(mix_d), mix_d], axis=3).reshape(2 * count, -1)
    mixed = dot_nn(
        jnp.concatenate([*split_three(mix_y), mix_d]), back.reshape(rings * 2 * slots, feature)
    ).reshape(4, 2, count, feature)
    sum_y = mixed[0] + mixed[1] + mixed[2]
    sum_d = mixed[3]
    theirs = jnp.concatenate([sum_y[1], sum_d[1]]).astype(BF16)
    ours = swap(theirs, "xh").astype(F32)
    layer_out = (sum_y[0] + ours[:count]).astype(BF16)
    input_grad = (sum_d[0] + ours[count:]).astype(BF16)
    return layer_out, input_grad, jnp.stack(updated[:2])[None], updated[2][None]


def solution(mesh):
    wide = Mesh(mesh.devices.reshape(2, 4, 8, 2, 2), ALL)
    token_spec = P(ALL, None)
    expert, share = ("xh", "y", "z"), ("xl", "core")
    up_spec = P(expert, None, share, None)
    down_spec = P(expert, share, None)
    return jax.shard_map(
        body,
        mesh=wide,
        in_specs=(token_spec, token_spec, token_spec, token_spec, P(), up_spec, down_spec, up_spec,
                  up_spec, down_spec, down_spec),
        out_specs=(token_spec, token_spec, up_spec, down_spec),
        check_vma=False,
    )
```

```python
import jax
import jax.numpy as jnp
from jax import lax
from jax.experimental import pallas as pl
from jax.experimental.pallas import tpu as pltpu
from jax.sharding import Mesh, PartitionSpec as P

BETA_ONE = 0.9
BETA_TWO = 0.95
STEP_RATE = 0.01
ADAM_EPS = 1e-08

F32 = jnp.float32
BF16 = jnp.bfloat16
CAP = 6
RINGS = ("y", "z")
ALL = ("xh", "y", "z", "xl", "core")


def swap(block, axis):
    return lax.ppermute(block, axis, [(0, 1), (1, 0)])


def after(value, *earlier):
    return lax.optimization_barrier((value, *earlier))[0]


def adam_update(weight, moment_one, moment_two, gradient):
    one_new = BETA_ONE * moment_one.astype(F32) + (1.0 - BETA_ONE) * gradient
    two_new = BETA_TWO * moment_two.astype(F32) + (1.0 - BETA_TWO) * gradient * gradient
    return (weight.astype(F32) - STEP_RATE * one_new / (jnp.sqrt(two_new) + ADAM_EPS)).astype(BF16)


def dot_nt(left, right):
    return lax.dot_general(left, right, (((1,), (1,)), ((), ())), preferred_element_type=F32)


def dot_nn(left, right):
    return lax.dot_general(left, right, (((1,), (0,)), ((), ())), preferred_element_type=F32)


def dot_tn(left, right):
    return lax.dot_general(left, right, (((0,), (0,)), ((), ())), preferred_element_type=F32)


CHUNK = 256
LANES = 512
GROUP = 16
VMEM_LIMIT = 56 * 1024 * 1024


def mixed_order(size):
    to = lax.broadcasted_iota(jnp.int32, (size, size), 0)
    at = lax.broadcasted_iota(jnp.int32, (size, size), 1)
    part = to // (size // 2)
    row = to - part * (size // 2)
    return (at == (row // 4) * 8 + part * 4 + row % 4).astype(BF16)


def rows_kernel(rows_ref, w_own, w_xl, w_pair, back_ref, xd_out, act_out, g_pair,
                w_all, xd, mixed, acts, g_all, w_sem, xd_sem, act_sem, g_sem):
    share = w_own.shape[1]
    width = 4 * share
    rows = xd.shape[1]
    pairs = rows_ref.shape[0] // (3 * GROUP)
    plain = pairs * GROUP
    sources = (w_pair.at[0], w_pair.at[1], w_own, w_xl)
    loads = [
        pltpu.make_async_copy(src, w_all.at[:, pl.ds(i * share, share)], w_sem.at[i])
        for i, src in enumerate(sources)
    ]
    for load in loads:
        load.start()

    upper = lax.broadcasted_iota(jnp.int32, (GROUP, rows_ref.shape[1]), 0) < GROUP // 2

    def part(p, carry):
        base = pl.multiple_of(p * 3 * GROUP, GROUP)
        first = rows_ref[pl.ds(base, GROUP), :]
        last = rows_ref[pl.ds(base + 2 * GROUP, GROUP), :]
        to = pl.ds(pl.multiple_of(p * GROUP, GROUP), GROUP)
        xd[0, to, :] = jnp.where(upper, first, last)
        xd[1, to, :] = rows_ref[pl.ds(base + GROUP, GROUP), :]
        mixed[to, :] = jnp.where(upper, last, first)
        return carry

    lax.fori_loop(0, pairs, part, 0)
    order = mixed_order(plain)
    for n in range(0, rows_ref.shape[1], LANES):
        sorted_rows = dot_nn(order, mixed[:, n:n + LANES]).astype(BF16)
        xd[0, plain:, n:n + LANES] = sorted_rows[:plain // 2]
        xd[1, plain:, n:n + LANES] = sorted_rows[plain // 2:]
    xd_store = pltpu.make_async_copy(xd, xd_out, xd_sem)
    xd_store.start()

    done = 0
    for f in range(0, width, CHUNK):
        while done * share < f + CHUNK:
            loads[done].wait()
            done += 1
        a = dot_nt(xd[0], w_all[0, f:f + CHUNK, :])
        u = dot_nt(xd[0], w_all[1, f:f + CHUNK, :])
        s = 1.0 / (1.0 + jnp.exp(-a))
        dh = dot_nt(xd[1], w_all[2, f:f + CHUNK, :])
        acts[2, :, f:f + CHUNK] = (a * s * u).astype(BF16)
        acts[0, :, f:f + CHUNK] = (dh * u * s * (1.0 + a * (1.0 - s))).astype(BF16)
        acts[1, :, f:f + CHUNK] = (dh * a * s).astype(BF16)
    act_store = pltpu.make_async_copy(acts.at[:, :, pl.ds(2 * share, 2 * share)], act_out, act_sem)
    act_store.start()

    stores = [
        pltpu.make_async_copy(g_all.at[:, pl.ds(i * share, share)], g_pair.at[i], g_sem.at[i])
        for i in range(2)
    ]
    for i, side in enumerate((0, 0, 1)):
        for n in range(0, rows_ref.shape[1], LANES):
            g_all[i, :, n:n + LANES] = dot_tn(
                acts[i, :, :2 * share], xd[side, :, n:n + LANES]
            ).astype(BF16)
    for store in stores:
        store.start()

    cut = lax.broadcasted_iota(jnp.int32, (GROUP, LANES), 0) < GROUP // 2
    for n in range(0, rows_ref.shape[1], LANES):
        o = dot_nn(acts[2], w_all[2, :, n:n + LANES]).astype(BF16)
        dx = (
            dot_nn(acts[0], w_all[0, :, n:n + LANES]) + dot_nn(acts[1], w_all[1, :, n:n + LANES])
        ).astype(BF16)
        blend = dot_tn(order, jnp.concatenate([o[plain:], dx[plain:]])).astype(BF16)
        for p in range(pairs):
            o_part = o[p * GROUP:(p + 1) * GROUP]
            m_part = blend[p * GROUP:(p + 1) * GROUP]
            base = p * 3 * GROUP
            back_ref[base:base + GROUP, n:n + LANES] = jnp.where(cut, o_part, m_part)
            back_ref[base + GROUP:base + 2 * GROUP, n:n + LANES] = dx[p * GROUP:(p + 1) * GROUP]
            back_ref[base + 2 * GROUP:base + 3 * GROUP, n:n + LANES] = jnp.where(cut, m_part, o_part)
    xd_store.wait()
    act_store.wait()
    for store in stores:
        store.wait()


def rows_step(rows, w_own, w_xl, w_pair):
    total, feature = rows.shape
    half = total // 2
    share = w_own.shape[1]
    any_spec = pl.BlockSpec(memory_space=pl.ANY)
    vmem_spec = pl.BlockSpec(memory_space=pltpu.VMEM)
    return pl.pallas_call(
        rows_kernel,
        out_shape=(
            jax.ShapeDtypeStruct(rows.shape, BF16),
            jax.ShapeDtypeStruct((2, half, feature), BF16),
            jax.ShapeDtypeStruct((3, half, 2 * share), BF16),
            jax.ShapeDtypeStruct(w_pair.shape, BF16),
        ),
        in_specs=[vmem_spec, any_spec, any_spec, any_spec],
        out_specs=(vmem_spec, any_spec, any_spec, any_spec),
        scratch_shapes=[
            pltpu.VMEM((3, 4 * share, feature), BF16),
            pltpu.VMEM((2, half, feature), BF16),
            pltpu.VMEM((total // 3, feature), BF16),
            pltpu.VMEM((3, half, 4 * share), BF16),
            pltpu.VMEM((3, 2 * share, feature), BF16),
            pltpu.SemaphoreType.DMA((4,)),
            pltpu.SemaphoreType.DMA,
            pltpu.SemaphoreType.DMA,
            pltpu.SemaphoreType.DMA((2,)),
        ],
        compiler_params=pltpu.CompilerParams(vmem_limit_bytes=VMEM_LIMIT),
        cost_estimate=pl.CostEstimate(
            flops=15 * half * feature * 4 * share,
            bytes_accessed=2 * (3 * total * feature + 18 * share * feature),
            transcendentals=half * 4 * share,
        ),
    )(rows, w_own, w_xl, w_pair)


def grads_kernel(flag_ref, xd_ref, act_ref, core_ref, *outs):
    share = core_ref.shape[2]
    moved = flag_ref[0] != 0
    for i, side in enumerate((0, 0, 1)):
        g = dot_tn(act_ref[i], xd_ref[side])
        own = g[:share] + core_ref[0, i].astype(F32)
        other = g[share:] + core_ref[1, i].astype(F32)
        if i < 2:
            own, other = jnp.where(moved, other, own), jnp.where(moved, own, other)
        outs[i][...] = own.astype(BF16)
        outs[3 + i][...] = other.astype(BF16)


def grads_step(flag, xd, acts, core):
    _, half, feature = xd.shape
    share = core.shape[2]
    out = jax.ShapeDtypeStruct((share, feature), BF16)
    return pl.pallas_call(
        grads_kernel,
        grid=(feature // LANES,),
        out_shape=(out,) * 6,
        in_specs=[
            pl.BlockSpec(memory_space=pltpu.SMEM),
            pl.BlockSpec((2, half, LANES), lambda n: (0, 0, n)),
            pl.BlockSpec(acts.shape, lambda n: (0, 0, 0)),
            pl.BlockSpec((2, 3, share, LANES), lambda n: (0, 0, 0, n)),
        ],
        out_specs=(pl.BlockSpec((share, LANES), lambda n: (0, n)),) * 6,
        compiler_params=pltpu.CompilerParams(vmem_limit_bytes=VMEM_LIMIT),
        cost_estimate=pl.CostEstimate(
            flops=12 * half * feature * share,
            bytes_accessed=2 * (2 * half * feature + 12 * share * feature),
            transcendentals=0,
        ),
    )(flag, xd, acts, core)


def adam_kernel(flag_ref, keep_ref, recv_ref, *refs):
    moved = flag_ref[0] != 0
    out_ref = refs[-1]
    if len(refs) == 7:
        w, m, v = [
            jnp.where(moved, refs[i + 3][...].astype(F32), refs[i][...].astype(F32)) for i in range(3)
        ]
    else:
        w, m, v = [ref[...].astype(F32) for ref in refs[:3]]
    gradient = keep_ref[...].astype(F32) + recv_ref[...].astype(F32)
    out_ref[...] = adam_update(w, m, v, gradient)


def adam_step(flag, *arrays):
    rows, feature = arrays[0].shape
    block = pl.BlockSpec((rows // 4, feature), lambda n: (n, 0))
    return pl.pallas_call(
        adam_kernel,
        grid=(4,),
        out_shape=jax.ShapeDtypeStruct((rows, feature), BF16),
        in_specs=[pl.BlockSpec(memory_space=pltpu.SMEM)] + [block] * len(arrays),
        out_specs=block,
        compiler_params=pltpu.CompilerParams(vmem_limit_bytes=VMEM_LIMIT),
        cost_estimate=pl.CostEstimate(
            flops=20 * rows * feature,
            bytes_accessed=2 * (len(arrays) + 1) * rows * feature,
            transcendentals=rows * feature,
        ),
    )(flag, *arrays)


def split_three(value):
    high = value.astype(BF16)
    rest = value - high.astype(F32)
    middle = rest.astype(BF16)
    low = (rest - middle.astype(F32)).astype(BF16)
    return high, middle, low


def body(tokens, cotangent, routes, route_weights, matching, gate_up, down, gate_up_m, gate_up_v,
         down_m, down_v):
    half = lax.axis_index("xh")
    rings = lax.axis_size("y") * lax.axis_size("z")
    ring = lax.axis_index("y") * lax.axis_size("z") + lax.axis_index("z")
    self_index = half * rings + ring
    swapped = jnp.sum(jnp.where(jnp.arange(2 * rings) == self_index, matching, 0)) != self_index
    flag = swapped.astype(jnp.int32).reshape(1)
    count, feature = tokens.shape
    slots = 2 * CAP

    top = routes.shape[1]
    named = jnp.concatenate([routes.astype(F32), route_weights], axis=1)
    named_other = swap(named, "xh")
    tokens_other = swap(tokens, "xh")
    cotangent_other = swap(cotangent, "xh")
    source = jnp.concatenate([tokens, cotangent, tokens_other, cotangent_other])

    w_own = jnp.concatenate([gate_up[0], down])
    w_first = after(w_own, tokens_other, cotangent_other, named_other)
    w_xl = swap(w_first, "xl")
    w_pair = swap(jnp.stack([w_own, w_xl]), "core")
    m_first, v_first, _ = lax.optimization_barrier((gate_up_m[0], gate_up_v[0], w_xl))
    m_xl = swap(m_first, "xl")
    v_xl = swap(v_first, "xl")

    both = jnp.stack([named, named_other])
    both_routes = both[:, :, :top].astype(jnp.int32)
    both_weights = both[:, :, top:]
    ring_ids = jnp.arange(rings, dtype=jnp.int32)[:, None, None]
    hit = [both_routes[:, :, k] == half * rings + ring_ids for k in range(top)]
    used = sum(h.astype(jnp.int32) for h in hit)
    scale = sum(jnp.where(h, both_weights[:, :, k], 0.0) for k, h in enumerate(hit))
    before = (jnp.arange(count)[:, None] < jnp.arange(count)[None, :]).astype(BF16)
    earlier = jnp.dot(used.astype(BF16), before, preferred_element_type=F32).astype(jnp.int32)
    slot = earlier + CAP * jnp.arange(2, dtype=jnp.int32)[None, :, None]
    slot = jnp.where(used > 0, slot, -1)

    def on_lanes(value):
        return jnp.concatenate([value[:, 0], value[:, 0], value[:, 1], value[:, 1]], axis=1)[:, None]

    lane_kind = jnp.arange(4 * count, dtype=jnp.int32) // count % 2
    row = jnp.arange(2 * slots, dtype=jnp.int32)
    row = jnp.where(ring % 2 == 0, row, jnp.where(row < 8, row + 16, jnp.where(row < 16, row, row - 16)))
    row_kind = (row >= 12).astype(jnp.int32)
    row_slot = jnp.where(row < 12, row, jnp.where(row < 16, row - 4, row - 16))
    pick = (on_lanes(slot) == row_slot[:, None]) & (lane_kind == row_kind[:, None])
    lane_scale = jnp.where(lane_kind == 0, on_lanes(scale), 1.0)
    row_scale = jnp.sum(jnp.where(pick, on_lanes(scale), 0.0), axis=2)
    factor = jnp.where(row_kind == 0, 1.0, row_scale).reshape(-1, 1)
    pick_b = pick.astype(BF16).reshape(rings * 2 * slots, 4 * count)
    send = (dot_nn(pick_b, source) * factor).astype(BF16).reshape(rings, 2 * slots, feature)

    recv = lax.all_to_all(send, RINGS, split_axis=0, concat_axis=0, tiled=True)
    back_send, xd, acts, g_pair = rows_step(recv.reshape(-1, feature), w_own, w_xl, w_pair)

    g_core = swap(g_pair, "core")
    back = lax.all_to_all(
        back_send.reshape(recv.shape), RINGS, split_axis=0, concat_axis=0, tiled=True
    ).reshape(-1, feature)
    parts = grads_step(flag, xd, acts, g_core)
    new_down = adam_step(flag, parts[2], swap(parts[5], "xl"), w_own[2], down_m[0], down_v[0])
    new_down = jnp.where(swapped, swap(new_down, "xh"), new_down)
    updated = []
    for i in range(2):
        new = adam_step(flag, parts[i], swap(parts[3 + i], "xl"), w_own[i], gate_up_m[0, i],
                        gate_up_v[0, i], w_xl[i], m_xl[i], v_xl[i])
        across = lax.ppermute(new, ("xh", "xl"), [(0, 3), (3, 0), (1, 2), (2, 1)])
        updated.append(jnp.where(swapped, across, new))

    mix = [
        jnp.where(pick, term, 0).reshape(rings * 2 * slots, 4 * count)
        for term in split_three(lane_scale)
    ]
    mixed = dot_tn(jnp.concatenate(mix, axis=1), back).reshape(3, 4 * count, feature)
    mixed = mixed[0] + mixed[1] + mixed[2]
    theirs = mixed[2 * count:].astype(BF16)
    ours = swap(theirs, "xh").astype(F32)
    layer_out = (mixed[:count] + ours[:count]).astype(BF16)
    input_grad = (mixed[count:2 * count] + ours[count:]).astype(BF16)
    return layer_out, input_grad, jnp.stack(updated)[None], new_down[None]


def solution(mesh):
    wide = Mesh(mesh.devices.reshape(2, 4, 8, 2, 2), ALL)
    token_spec = P(ALL, None)
    expert, share = ("xh", "y", "z"), ("xl", "core")
    up_spec = P(expert, None, share, None)
    down_spec = P(expert, share, None)
    return jax.shard_map(
        body,
        mesh=wide,
        in_specs=(token_spec, token_spec, token_spec, token_spec, P(), up_spec, down_spec, up_spec,
                  up_spec, down_spec, down_spec),
        out_specs=(token_spec, token_spec, up_spec, down_spec),
        check_vma=False,
    )
```

```python
import jax
import jax.numpy as jnp
from jax import lax
from jax.experimental import pallas as pl
from jax.experimental.pallas import tpu as pltpu
from jax.sharding import Mesh, PartitionSpec as P

BETA_ONE = 0.9
BETA_TWO = 0.95
STEP_RATE = 0.01
ADAM_EPS = 1e-08

F32 = jnp.float32
BF16 = jnp.bfloat16
CAP = 6
RINGS = ("y", "z")
ALL = ("xh", "y", "z", "xl", "core")


def swap(block, axis):
    return lax.ppermute(block, axis, [(0, 1), (1, 0)])


def after(value, *earlier):
    return lax.optimization_barrier((value, *earlier))[0]


def adam_update(weight, moment_one, moment_two, gradient):
    one_new = BETA_ONE * moment_one.astype(F32) + (1.0 - BETA_ONE) * gradient
    two_new = BETA_TWO * moment_two.astype(F32) + (1.0 - BETA_TWO) * gradient * gradient
    return (weight.astype(F32) - STEP_RATE * one_new / (jnp.sqrt(two_new) + ADAM_EPS)).astype(BF16)


def dot_nt(left, right):
    return lax.dot_general(left, right, (((1,), (1,)), ((), ())), preferred_element_type=F32)


def dot_nn(left, right):
    return lax.dot_general(left, right, (((1,), (0,)), ((), ())), preferred_element_type=F32)


def dot_tn(left, right):
    return lax.dot_general(left, right, (((0,), (0,)), ((), ())), preferred_element_type=F32)


CHUNK = 256
LANES = 512
GROUP = 16
VMEM_LIMIT = 56 * 1024 * 1024


def mixed_order(size):
    to = lax.broadcasted_iota(jnp.int32, (size, size), 0)
    at = lax.broadcasted_iota(jnp.int32, (size, size), 1)
    part = to // (size // 2)
    row = to - part * (size // 2)
    return (at == (row // 4) * 8 + part * 4 + row % 4).astype(BF16)


def rows_kernel(rows_ref, w_own, w_xl, w_pair, back_ref, xd_out, act_out, g_gate, g_up, g_down,
                w_all, xd, mixed, acts, g_all, w_sem, xd_sem, act_sem, g_sem):
    share = w_own.shape[1]
    width = 4 * share
    rows = xd.shape[1]
    pairs = rows_ref.shape[0] // (3 * GROUP)
    plain = pairs * GROUP
    sources = (w_pair.at[0], w_pair.at[1], w_own, w_xl)
    loads = [
        pltpu.make_async_copy(src, w_all.at[:, pl.ds(i * share, share)], w_sem.at[i])
        for i, src in enumerate(sources)
    ]
    for load in loads:
        load.start()

    upper = lax.broadcasted_iota(jnp.int32, (GROUP, rows_ref.shape[1]), 0) < GROUP // 2

    def part(p, carry):
        base = pl.multiple_of(p * 3 * GROUP, GROUP)
        first = rows_ref[pl.ds(base, GROUP), :]
        last = rows_ref[pl.ds(base + 2 * GROUP, GROUP), :]
        to = pl.ds(pl.multiple_of(p * GROUP, GROUP), GROUP)
        xd[0, to, :] = jnp.where(upper, first, last)
        xd[1, to, :] = rows_ref[pl.ds(base + GROUP, GROUP), :]
        mixed[to, :] = jnp.where(upper, last, first)
        return carry

    lax.fori_loop(0, pairs, part, 0)
    order = mixed_order(plain)
    for n in range(0, rows_ref.shape[1], LANES):
        sorted_rows = dot_nn(order, mixed[:, n:n + LANES]).astype(BF16)
        xd[0, plain:, n:n + LANES] = sorted_rows[:plain // 2]
        xd[1, plain:, n:n + LANES] = sorted_rows[plain // 2:]
    xd_store = pltpu.make_async_copy(xd, xd_out, xd_sem)
    xd_store.start()

    done = 0
    for f in range(0, width, CHUNK):
        while done * share < f + CHUNK:
            loads[done].wait()
            done += 1
        a = dot_nt(xd[0], w_all[0, f:f + CHUNK, :])
        u = dot_nt(xd[0], w_all[1, f:f + CHUNK, :])
        s = 1.0 / (1.0 + jnp.exp(-a))
        dh = dot_nt(xd[1], w_all[2, f:f + CHUNK, :])
        acts[2, :, f:f + CHUNK] = (a * s * u).astype(BF16)
        acts[0, :, f:f + CHUNK] = (dh * u * s * (1.0 + a * (1.0 - s))).astype(BF16)
        acts[1, :, f:f + CHUNK] = (dh * a * s).astype(BF16)
    act_store = pltpu.make_async_copy(acts.at[:, :, pl.ds(2 * share, 2 * share)], act_out, act_sem)
    act_store.start()

    stores = []
    for i, (side, target) in enumerate(zip((0, 0, 1), (g_gate, g_up, g_down))):
        for n in range(0, rows_ref.shape[1], LANES):
            g_all[i, :, n:n + LANES] = dot_tn(
                acts[i, :, :2 * share], xd[side, :, n:n + LANES]
            ).astype(BF16)
        stores.append(pltpu.make_async_copy(g_all.at[i], target, g_sem.at[i]))
        stores[i].start()

    cut = lax.broadcasted_iota(jnp.int32, (GROUP, LANES), 0) < GROUP // 2
    for n in range(0, rows_ref.shape[1], LANES):
        o = dot_nn(acts[2], w_all[2, :, n:n + LANES]).astype(BF16)
        dx = (
            dot_nn(acts[0], w_all[0, :, n:n + LANES]) + dot_nn(acts[1], w_all[1, :, n:n + LANES])
        ).astype(BF16)
        blend = dot_tn(order, jnp.concatenate([o[plain:], dx[plain:]])).astype(BF16)
        for p in range(pairs):
            o_part = o[p * GROUP:(p + 1) * GROUP]
            m_part = blend[p * GROUP:(p + 1) * GROUP]
            base = p * 3 * GROUP
            back_ref[base:base + GROUP, n:n + LANES] = jnp.where(cut, o_part, m_part)
            back_ref[base + GROUP:base + 2 * GROUP, n:n + LANES] = dx[p * GROUP:(p + 1) * GROUP]
            back_ref[base + 2 * GROUP:base + 3 * GROUP, n:n + LANES] = jnp.where(cut, m_part, o_part)
    xd_store.wait()
    act_store.wait()
    for store in stores:
        store.wait()


def rows_step(rows, w_own, w_xl, w_pair):
    total, feature = rows.shape
    half = total // 2
    share = w_own.shape[1]
    any_spec = pl.BlockSpec(memory_space=pl.ANY)
    vmem_spec = pl.BlockSpec(memory_space=pltpu.VMEM)
    return pl.pallas_call(
        rows_kernel,
        out_shape=(
            jax.ShapeDtypeStruct(rows.shape, BF16),
            jax.ShapeDtypeStruct((2, half, feature), BF16),
            jax.ShapeDtypeStruct((3, half, 2 * share), BF16),
        ) + (jax.ShapeDtypeStruct((2 * share, feature), BF16),) * 3,
        in_specs=[vmem_spec, any_spec, any_spec, any_spec],
        out_specs=(vmem_spec,) + (any_spec,) * 5,
        scratch_shapes=[
            pltpu.VMEM((3, 4 * share, feature), BF16),
            pltpu.VMEM((2, half, feature), BF16),
            pltpu.VMEM((total // 3, feature), BF16),
            pltpu.VMEM((3, half, 4 * share), BF16),
            pltpu.VMEM((3, 2 * share, feature), BF16),
            pltpu.SemaphoreType.DMA((4,)),
            pltpu.SemaphoreType.DMA,
            pltpu.SemaphoreType.DMA,
            pltpu.SemaphoreType.DMA((3,)),
        ],
        compiler_params=pltpu.CompilerParams(vmem_limit_bytes=VMEM_LIMIT),
        cost_estimate=pl.CostEstimate(
            flops=half * feature * share,
            bytes_accessed=half * feature,
            transcendentals=0,
        ),
    )(rows, w_own, w_xl, w_pair)


def grads_kernel(flag_ref, xd_ref, act_ref, core_gate, core_up, core_down, _mv_ref, *outs):
    share = core_gate.shape[0] // 2
    moved = flag_ref[0] != 0
    for i, (side, core_ref) in enumerate(zip((0, 0, 1), (core_gate, core_up, core_down))):
        g = dot_tn(act_ref[i], xd_ref[side]) + core_ref[...].astype(F32)
        own = g[:share]
        other = g[share:]
        if i < 2:
            own, other = jnp.where(moved, other, own), jnp.where(moved, own, other)
        outs[i][...] = own.astype(BF16)
        outs[3 + i][...] = other.astype(BF16)


def grads_step(flag, xd, acts, core, mv_xl):
    _, half, feature = xd.shape
    share = core[0].shape[0] // 2
    out = jax.ShapeDtypeStruct((share, feature), BF16)
    return pl.pallas_call(
        grads_kernel,
        grid=(feature // LANES,),
        out_shape=(out,) * 6,
        in_specs=[
            pl.BlockSpec(memory_space=pltpu.SMEM),
            pl.BlockSpec((2, half, LANES), lambda n: (0, 0, n)),
            pl.BlockSpec(acts.shape, lambda n: (0, 0, 0)),
            *[pl.BlockSpec((2 * share, LANES), lambda n: (0, n))] * 3,
            pl.BlockSpec(memory_space=pl.ANY),
        ],
        out_specs=(pl.BlockSpec((share, LANES), lambda n: (0, n)),) * 6,
        compiler_params=pltpu.CompilerParams(vmem_limit_bytes=VMEM_LIMIT),
        cost_estimate=pl.CostEstimate(
            flops=12 * half * feature * share,
            bytes_accessed=2 * (2 * half * feature + 12 * share * feature),
            transcendentals=0,
        ),
    )(flag, xd, acts, *core, mv_xl)


def adam_kernel(flag_ref, keep_ref, recv_ref, *refs):
    moved = flag_ref[0] != 0
    out_ref = refs[-1]
    if len(refs) == 7:
        w, m, v = [
            jnp.where(moved, refs[i + 3][...].astype(F32), refs[i][...].astype(F32)) for i in range(3)
        ]
    else:
        w, m, v = [ref[...].astype(F32) for ref in refs[:3]]
    gradient = keep_ref[...].astype(F32) + recv_ref[...].astype(F32)
    out_ref[...] = adam_update(w, m, v, gradient)


def adam_step(flag, *arrays):
    rows, feature = arrays[0][0].shape[-2:]
    steps = 4

    def spec(lead):
        return pl.BlockSpec((None,) * len(lead) + (rows // steps, feature), lambda n: (*lead, n, 0))

    return pl.pallas_call(
        adam_kernel,
        grid=(steps,),
        out_shape=jax.ShapeDtypeStruct((rows, feature), BF16),
        in_specs=[pl.BlockSpec(memory_space=pltpu.SMEM)] + [spec(lead) for _, lead in arrays],
        out_specs=spec(()),
        compiler_params=pltpu.CompilerParams(vmem_limit_bytes=VMEM_LIMIT),
        cost_estimate=pl.CostEstimate(
            flops=20 * rows * feature,
            bytes_accessed=2 * (len(arrays) + 1) * rows * feature,
            transcendentals=rows * feature,
        ),
    )(flag, *[array for array, _ in arrays])


def split_three(value):
    high = value.astype(BF16)
    rest = value - high.astype(F32)
    middle = rest.astype(BF16)
    low = (rest - middle.astype(F32)).astype(BF16)
    return high, middle, low


def body(tokens, cotangent, routes, route_weights, matching, gate_up, down, gate_up_m, gate_up_v,
         down_m, down_v):
    half = lax.axis_index("xh")
    rings = lax.axis_size("y") * lax.axis_size("z")
    ring = lax.axis_index("y") * lax.axis_size("z") + lax.axis_index("z")
    self_index = half * rings + ring
    swapped = jnp.sum(jnp.where(jnp.arange(2 * rings) == self_index, matching, 0)) != self_index
    flag = swapped.astype(jnp.int32).reshape(1)
    count, feature = tokens.shape
    slots = 2 * CAP

    top = routes.shape[1]
    named = jnp.concatenate([routes.astype(F32), route_weights], axis=1)
    named_other = swap(named, "xh")
    tokens_other = swap(tokens, "xh")
    cotangent_other = swap(cotangent, "xh")
    source = jnp.concatenate([tokens, cotangent, tokens_other, cotangent_other])

    w_own = jnp.concatenate([gate_up[0], down])
    w_first = after(w_own, tokens_other, cotangent_other, named_other)
    w_xl = swap(w_first, "xl")
    w_pair = swap(jnp.stack([w_own, w_xl]), "core")
    mv_xl = swap(after(jnp.concatenate([gate_up_m[0], gate_up_v[0]]), w_xl), "xl")

    both = jnp.stack([named, named_other])
    both_routes = both[:, :, :top].astype(jnp.int32)
    both_weights = both[:, :, top:]
    ring_ids = jnp.arange(rings, dtype=jnp.int32)[:, None, None]
    hit = [both_routes[:, :, k] == half * rings + ring_ids for k in range(top)]
    used = sum(h.astype(jnp.int32) for h in hit)
    scale = sum(jnp.where(h, both_weights[:, :, k], 0.0) for k, h in enumerate(hit))
    before = (jnp.arange(count)[:, None] < jnp.arange(count)[None, :]).astype(BF16)
    earlier = jnp.dot(used.astype(BF16), before, preferred_element_type=F32).astype(jnp.int32)
    slot = earlier + CAP * jnp.arange(2, dtype=jnp.int32)[None, :, None]
    slot = jnp.where(used > 0, slot, -1)

    def on_lanes(value):
        return jnp.concatenate([value[:, 0], value[:, 0], value[:, 1], value[:, 1]], axis=1)[:, None]

    lane_kind = jnp.arange(4 * count, dtype=jnp.int32) // count % 2
    row = jnp.arange(2 * slots, dtype=jnp.int32)
    row = jnp.where(ring % 2 == 0, row, jnp.where(row < 8, row + 16, jnp.where(row < 16, row, row - 16)))
    row_kind = (row >= 12).astype(jnp.int32)
    row_slot = jnp.where(row < 12, row, jnp.where(row < 16, row - 4, row - 16))
    pick = (on_lanes(slot) == row_slot[:, None]) & (lane_kind == row_kind[:, None])
    lane_scale = jnp.where(lane_kind == 0, on_lanes(scale), 1.0)
    row_scale = jnp.sum(jnp.where(pick, on_lanes(scale), 0.0), axis=2)
    factor = jnp.where(row_kind == 0, 1.0, row_scale).reshape(-1, 1)
    pick_b = pick.astype(BF16).reshape(rings * 2 * slots, 4 * count)
    send = (dot_nn(pick_b, source) * factor).astype(BF16).reshape(rings, 2 * slots, feature)

    recv = lax.all_to_all(send, RINGS, split_axis=0, concat_axis=0, tiled=True)
    back_send, xd, acts, *g_pair = rows_step(recv.reshape(-1, feature), w_own, w_xl, w_pair)

    g_core = [swap(g, "core") for g in g_pair]
    back = lax.all_to_all(
        back_send.reshape(recv.shape), RINGS, split_axis=0, concat_axis=0, tiled=True
    ).reshape(-1, feature)
    parts = grads_step(flag, xd, acts, g_core, mv_xl)
    new_down = adam_step(flag, (parts[2], ()), (swap(parts[5], "xl"), ()), (down, (0,)), (down_m, (0,)),
                         (down_v, (0,)))
    new_down = jnp.where(swapped, swap(new_down, "xh"), new_down)
    updated = []
    for i in range(2):
        new = adam_step(flag, (parts[i], ()), (swap(parts[3 + i], "xl"), ()), (gate_up, (0, i)),
                        (gate_up_m, (0, i)), (gate_up_v, (0, i)), (w_xl, (i,)), (mv_xl, (i,)),
                        (mv_xl, (2 + i,)))
        across = lax.ppermute(new, ("xh", "xl"), [(0, 3), (3, 0), (1, 2), (2, 1)])
        updated.append(jnp.where(swapped, across, new))

    mix = [
        jnp.where(pick, term, 0).reshape(rings * 2 * slots, 4 * count)
        for term in split_three(lane_scale)
    ]
    mixed = dot_tn(jnp.concatenate(mix, axis=1), back).reshape(3, 4 * count, feature)
    mixed = mixed[0] + mixed[1] + mixed[2]
    theirs = mixed[2 * count:].astype(BF16)
    ours = swap(theirs, "xh").astype(F32)
    layer_out = (mixed[:count] + ours[:count]).astype(BF16)
    input_grad = (mixed[count:2 * count] + ours[count:]).astype(BF16)
    return layer_out, input_grad, jnp.stack(updated)[None], new_down[None]


def solution(mesh):
    wide = Mesh(mesh.devices.reshape(2, 4, 8, 2, 2), ALL)
    token_spec = P(ALL, None)
    expert, share = ("xh", "y", "z"), ("xl", "core")
    up_spec = P(expert, None, share, None)
    down_spec = P(expert, share, None)
    return jax.shard_map(
        body,
        mesh=wide,
        in_specs=(token_spec, token_spec, token_spec, token_spec, P(), up_spec, down_spec, up_spec,
                  up_spec, down_spec, down_spec),
        out_specs=(token_spec, token_spec, up_spec, down_spec),
        check_vma=False,
    )
```

```python
import jax
import jax.numpy as jnp
from jax import lax
from jax.experimental import pallas as pl
from jax.experimental.pallas import tpu as pltpu
from jax.sharding import Mesh, PartitionSpec as P

BETA_ONE = 0.9
BETA_TWO = 0.95
STEP_RATE = 0.01
ADAM_EPS = 1e-08

F32 = jnp.float32
BF16 = jnp.bfloat16
CAP = 6
RINGS = ("y", "z")
ALL = ("xh", "y", "z", "xl", "core")


def swap(block, axis):
    return lax.ppermute(block, axis, [(0, 1), (1, 0)])


def after(value, *earlier):
    return lax.optimization_barrier((value, *earlier))[0]


def adam_update(weight, moment_one, moment_two, gradient):
    one_new = BETA_ONE * moment_one.astype(F32) + (1.0 - BETA_ONE) * gradient
    two_new = BETA_TWO * moment_two.astype(F32) + (1.0 - BETA_TWO) * gradient * gradient
    return (weight.astype(F32) - STEP_RATE * one_new / (jnp.sqrt(two_new) + ADAM_EPS)).astype(BF16)


def dot_nt(left, right):
    return lax.dot_general(left, right, (((1,), (1,)), ((), ())), preferred_element_type=F32)


def dot_nn(left, right):
    return lax.dot_general(left, right, (((1,), (0,)), ((), ())), preferred_element_type=F32)


def dot_tn(left, right):
    return lax.dot_general(left, right, (((0,), (0,)), ((), ())), preferred_element_type=F32)


CHUNK = 256
LANES = 512
GROUP = 16
VMEM_LIMIT = 56 * 1024 * 1024


def mixed_order(size):
    to = lax.broadcasted_iota(jnp.int32, (size, size), 0)
    at = lax.broadcasted_iota(jnp.int32, (size, size), 1)
    part = to // (size // 2)
    row = to - part * (size // 2)
    return (at == (row // 4) * 8 + part * 4 + row % 4).astype(BF16)


def rows_kernel(rows_ref, w_own, w_xl, w_pair, _mv, back_ref, xd_out, act_out, g_gate, g_up, g_down,
                w_all, xd, mixed, acts, g_all, w_sem, xd_sem, act_sem, g_sem):
    share = w_own.shape[1]
    width = 4 * share
    rows = xd.shape[1]
    pairs = rows_ref.shape[0] // (3 * GROUP)
    plain = pairs * GROUP
    sources = (w_pair.at[0], w_pair.at[1], w_own, w_xl)
    loads = [
        pltpu.make_async_copy(src, w_all.at[:, pl.ds(i * share, share)], w_sem.at[i])
        for i, src in enumerate(sources)
    ]
    for load in loads:
        load.start()

    upper = lax.broadcasted_iota(jnp.int32, (GROUP, rows_ref.shape[1]), 0) < GROUP // 2

    def part(p, carry):
        base = pl.multiple_of(p * 3 * GROUP, GROUP)
        first = rows_ref[pl.ds(base, GROUP), :]
        last = rows_ref[pl.ds(base + 2 * GROUP, GROUP), :]
        to = pl.ds(pl.multiple_of(p * GROUP, GROUP), GROUP)
        xd[0, to, :] = jnp.where(upper, first, last)
        xd[1, to, :] = rows_ref[pl.ds(base + GROUP, GROUP), :]
        mixed[to, :] = jnp.where(upper, last, first)
        return carry

    lax.fori_loop(0, pairs, part, 0)
    order = mixed_order(plain)
    for n in range(0, rows_ref.shape[1], LANES):
        sorted_rows = dot_nn(order, mixed[:, n:n + LANES]).astype(BF16)
        xd[0, plain:, n:n + LANES] = sorted_rows[:plain // 2]
        xd[1, plain:, n:n + LANES] = sorted_rows[plain // 2:]
    xd_store = pltpu.make_async_copy(xd, xd_out, xd_sem)
    xd_store.start()

    done = 0
    for f in range(0, width, CHUNK):
        while done * share < f + CHUNK:
            loads[done].wait()
            done += 1
        a = dot_nt(xd[0], w_all[0, f:f + CHUNK, :])
        u = dot_nt(xd[0], w_all[1, f:f + CHUNK, :])
        s = 1.0 / (1.0 + jnp.exp(-a))
        dh = dot_nt(xd[1], w_all[2, f:f + CHUNK, :])
        acts[2, :, f:f + CHUNK] = (a * s * u).astype(BF16)
        acts[0, :, f:f + CHUNK] = (dh * u * s * (1.0 + a * (1.0 - s))).astype(BF16)
        acts[1, :, f:f + CHUNK] = (dh * a * s).astype(BF16)
    act_store = pltpu.make_async_copy(acts.at[:, :, pl.ds(2 * share, 2 * share)], act_out, act_sem)
    act_store.start()

    stores = []
    for i, (side, target) in enumerate(zip((0, 0, 1), (g_gate, g_up, g_down))):
        for n in range(0, rows_ref.shape[1], LANES):
            g_all[i, :, n:n + LANES] = dot_tn(
                acts[i, :, :2 * share], xd[side, :, n:n + LANES]
            ).astype(BF16)
        stores.append(pltpu.make_async_copy(g_all.at[i], target, g_sem.at[i]))
        stores[i].start()

    cut = lax.broadcasted_iota(jnp.int32, (GROUP, LANES), 0) < GROUP // 2
    for n in range(0, rows_ref.shape[1], LANES):
        o = dot_nn(acts[2], w_all[2, :, n:n + LANES]).astype(BF16)
        dx = (
            dot_nn(acts[0], w_all[0, :, n:n + LANES]) + dot_nn(acts[1], w_all[1, :, n:n + LANES])
        ).astype(BF16)
        blend = dot_tn(order, jnp.concatenate([o[plain:], dx[plain:]])).astype(BF16)
        for p in range(pairs):
            o_part = o[p * GROUP:(p + 1) * GROUP]
            m_part = blend[p * GROUP:(p + 1) * GROUP]
            base = p * 3 * GROUP
            back_ref[base:base + GROUP, n:n + LANES] = jnp.where(cut, o_part, m_part)
            back_ref[base + GROUP:base + 2 * GROUP, n:n + LANES] = dx[p * GROUP:(p + 1) * GROUP]
            back_ref[base + 2 * GROUP:base + 3 * GROUP, n:n + LANES] = jnp.where(cut, m_part, o_part)
    xd_store.wait()
    act_store.wait()
    for store in stores:
        store.wait()


def rows_step(rows, w_own, w_xl, w_pair, mv_xl):
    total, feature = rows.shape
    half = total // 2
    share = w_own.shape[1]
    any_spec = pl.BlockSpec(memory_space=pl.ANY)
    vmem_spec = pl.BlockSpec(memory_space=pltpu.VMEM)
    return pl.pallas_call(
        rows_kernel,
        out_shape=(
            jax.ShapeDtypeStruct(rows.shape, BF16),
            jax.ShapeDtypeStruct((2, half, feature), BF16),
            jax.ShapeDtypeStruct((3, half, 2 * share), BF16),
        ) + (jax.ShapeDtypeStruct((2 * share, feature), BF16),) * 3,
        in_specs=[vmem_spec] + [any_spec] * 4,
        out_specs=(vmem_spec,) + (any_spec,) * 5,
        scratch_shapes=[
            pltpu.VMEM((3, 4 * share, feature), BF16),
            pltpu.VMEM((2, half, feature), BF16),
            pltpu.VMEM((total // 3, feature), BF16),
            pltpu.VMEM((3, half, 4 * share), BF16),
            pltpu.VMEM((3, 2 * share, feature), BF16),
            pltpu.SemaphoreType.DMA((4,)),
            pltpu.SemaphoreType.DMA,
            pltpu.SemaphoreType.DMA,
            pltpu.SemaphoreType.DMA((3,)),
        ],
        compiler_params=pltpu.CompilerParams(vmem_limit_bytes=VMEM_LIMIT),
        cost_estimate=pl.CostEstimate(
            flops=half * feature * share,
            bytes_accessed=half * feature,
            transcendentals=0,
        ),
    )(rows, w_own, w_xl, w_pair, mv_xl)


def grads_kernel(flag_ref, xd_ref, act_ref, core_gate, core_up, core_down, *outs):
    share = core_gate.shape[0] // 2
    moved = flag_ref[0] != 0
    for i, (side, core_ref) in enumerate(zip((0, 0, 1), (core_gate, core_up, core_down))):
        g = dot_tn(act_ref[i], xd_ref[side]) + core_ref[...].astype(F32)
        own = g[:share]
        other = g[share:]
        if i < 1:
            own, other = jnp.where(moved, other, own), jnp.where(moved, own, other)
        outs[i][...] = own.astype(BF16)
        outs[3 + i][...] = other.astype(BF16)


def grads_step(flag, xd, acts, core):
    _, half, feature = xd.shape
    share = core[0].shape[0] // 2
    out = jax.ShapeDtypeStruct((share, feature), BF16)
    return pl.pallas_call(
        grads_kernel,
        grid=(feature // LANES,),
        out_shape=(out,) * 6,
        in_specs=[
            pl.BlockSpec(memory_space=pltpu.SMEM),
            pl.BlockSpec((2, half, LANES), lambda n: (0, 0, n)),
            pl.BlockSpec(acts.shape, lambda n: (0, 0, 0)),
            *[pl.BlockSpec((2 * share, LANES), lambda n: (0, n))] * 3,
        ],
        out_specs=(pl.BlockSpec((share, LANES), lambda n: (0, n)),) * 6,
        compiler_params=pltpu.CompilerParams(vmem_limit_bytes=VMEM_LIMIT),
        cost_estimate=pl.CostEstimate(
            flops=12 * half * feature * share,
            bytes_accessed=2 * (2 * half * feature + 12 * share * feature),
            transcendentals=0,
        ),
    )(flag, xd, acts, *core)


def adam_kernel(flag_ref, keep_ref, recv_ref, *refs):
    moved = flag_ref[0] != 0
    out_ref = refs[-1]
    if len(refs) == 7:
        w, m, v = [
            jnp.where(moved, refs[i + 3][...].astype(F32), refs[i][...].astype(F32)) for i in range(3)
        ]
    else:
        w, m, v = [ref[...].astype(F32) for ref in refs[:3]]
    gradient = keep_ref[...].astype(F32) + recv_ref[...].astype(F32)
    out_ref[...] = adam_update(w, m, v, gradient)


def adam_step(flag, *arrays):
    rows, feature = arrays[0][0].shape[-2:]
    steps = 4

    def spec(lead):
        return pl.BlockSpec((None,) * len(lead) + (rows // steps, feature), lambda n: (*lead, n, 0))

    return pl.pallas_call(
        adam_kernel,
        grid=(steps,),
        out_shape=jax.ShapeDtypeStruct((rows, feature), BF16),
        in_specs=[pl.BlockSpec(memory_space=pltpu.SMEM)] + [spec(lead) for _, lead in arrays],
        out_specs=spec(()),
        compiler_params=pltpu.CompilerParams(vmem_limit_bytes=VMEM_LIMIT),
        cost_estimate=pl.CostEstimate(
            flops=20 * rows * feature,
            bytes_accessed=2 * (len(arrays) + 1) * rows * feature,
            transcendentals=rows * feature,
        ),
    )(flag, *[array for array, _ in arrays])


def settle_kernel(flag_ref, *refs):
    moved = flag_ref[0] != 0
    for i in range(refs[-1].shape[0]):
        refs[-1][i] = jnp.where(moved, refs[2 * i + 1][...], refs[2 * i][...])


def settle(flag, arrays, ready):
    rows, feature = arrays[0].shape
    count = len(arrays) // 2
    steps = 2
    block = pl.BlockSpec((rows // steps, feature), lambda n: (n, 0))
    return pl.pallas_call(
        settle_kernel,
        grid=(steps,),
        out_shape=jax.ShapeDtypeStruct((count, rows, feature), BF16),
        in_specs=[pl.BlockSpec(memory_space=pltpu.SMEM)] + [block] * len(arrays)
        + [pl.BlockSpec(memory_space=pl.ANY)],
        out_specs=pl.BlockSpec((count, rows // steps, feature), lambda n: (0, n, 0)),
        compiler_params=pltpu.CompilerParams(vmem_limit_bytes=VMEM_LIMIT),
        cost_estimate=pl.CostEstimate(
            flops=count * rows * feature, bytes_accessed=6 * count * rows * feature, transcendentals=0
        ),
    )(flag, *arrays, ready)


def split_three(value):
    high = value.astype(BF16)
    rest = value - high.astype(F32)
    middle = rest.astype(BF16)
    low = (rest - middle.astype(F32)).astype(BF16)
    return high, middle, low


def body(tokens, cotangent, routes, route_weights, matching, gate_up, down, gate_up_m, gate_up_v,
         down_m, down_v):
    half = lax.axis_index("xh")
    rings = lax.axis_size("y") * lax.axis_size("z")
    ring = lax.axis_index("y") * lax.axis_size("z") + lax.axis_index("z")
    self_index = half * rings + ring
    swapped = jnp.sum(jnp.where(jnp.arange(2 * rings) == self_index, matching, 0)) != self_index
    flag = swapped.astype(jnp.int32).reshape(1)
    count, feature = tokens.shape
    slots = 2 * CAP

    top = routes.shape[1]
    named = jnp.concatenate([routes.astype(F32), route_weights], axis=1)
    named_other = swap(named, "xh")
    tokens_other = swap(tokens, "xh")
    cotangent_other = swap(cotangent, "xh")
    source = jnp.concatenate([tokens, cotangent, tokens_other, cotangent_other])

    w_own = jnp.concatenate([gate_up[0], down])
    w_first = after(w_own, tokens_other, cotangent_other, named_other)
    w_xl = swap(w_first, "xl")
    w_pair = swap(jnp.stack([w_own, w_xl]), "core")
    mv_xl = swap(after(jnp.concatenate([gate_up_m[0, :1], gate_up_v[0, :1]]), w_xl), "xl")

    both = jnp.stack([named, named_other])
    both_routes = both[:, :, :top].astype(jnp.int32)
    both_weights = both[:, :, top:]
    ring_ids = jnp.arange(rings, dtype=jnp.int32)[:, None, None]
    hit = [both_routes[:, :, k] == half * rings + ring_ids for k in range(top)]
    used = sum(h.astype(jnp.int32) for h in hit)
    scale = sum(jnp.where(h, both_weights[:, :, k], 0.0) for k, h in enumerate(hit))
    before = (jnp.arange(count)[:, None] < jnp.arange(count)[None, :]).astype(BF16)
    earlier = jnp.dot(used.astype(BF16), before, preferred_element_type=F32).astype(jnp.int32)
    slot = earlier + CAP * jnp.arange(2, dtype=jnp.int32)[None, :, None]
    slot = jnp.where(used > 0, slot, -1)

    def on_lanes(value):
        return jnp.concatenate([value[:, 0], value[:, 0], value[:, 1], value[:, 1]], axis=1)[:, None]

    lane_kind = jnp.arange(4 * count, dtype=jnp.int32) // count % 2
    row = jnp.arange(2 * slots, dtype=jnp.int32)
    row = jnp.where(ring % 2 == 0, row, jnp.where(row < 8, row + 16, jnp.where(row < 16, row, row - 16)))
    row_kind = (row >= 12).astype(jnp.int32)
    row_slot = jnp.where(row < 12, row, jnp.where(row < 16, row - 4, row - 16))
    pick = (on_lanes(slot) == row_slot[:, None]) & (lane_kind == row_kind[:, None])
    lane_scale = jnp.where(lane_kind == 0, on_lanes(scale), 1.0)
    row_scale = jnp.sum(jnp.where(pick, on_lanes(scale), 0.0), axis=2)
    factor = jnp.where(row_kind == 0, 1.0, row_scale).reshape(-1, 1)
    pick_b = pick.astype(BF16).reshape(rings * 2 * slots, 4 * count)
    send = (dot_nn(pick_b, source) * factor).astype(BF16).reshape(rings, 2 * slots, feature)

    recv = lax.all_to_all(send, RINGS, split_axis=0, concat_axis=0, tiled=True)
    back_send, xd, acts, *g_pair = rows_step(recv.reshape(-1, feature), w_own, w_xl, w_pair, mv_xl)

    g_core = [swap(g, "core") for g in g_pair]
    back = lax.all_to_all(
        back_send.reshape(recv.shape), RINGS, split_axis=0, concat_axis=0, tiled=True
    ).reshape(-1, feature)
    parts = grads_step(flag, xd, acts, g_core)
    others = [swap(parts[3], "xl"), swap(parts[4], "xl")]
    new_gate = adam_step(flag, (parts[0], ()), (others[0], ()), (gate_up, (0, 0)), (gate_up_m, (0, 0)),
                         (gate_up_v, (0, 0)), (w_xl, (0,)), (mv_xl, (0,)), (mv_xl, (1,)))
    others.append(swap(after(parts[5], new_gate), "xl"))
    gate_other = lax.ppermute(new_gate, ("xh", "xl"), [(0, 3), (3, 0), (1, 2), (2, 1)])
    new_up = adam_step(flag, (parts[1], ()), (others[1], ()), (gate_up, (0, 1)), (gate_up_m, (0, 1)),
                       (gate_up_v, (0, 1)))
    arrived = [new_gate, gate_other, new_up, swap(new_up, "xh")]
    new_gate_up = settle(flag, arrived, mv_xl)
    new_down = adam_step(flag, (parts[2], ()), (others[2], ()), (down, (0,)), (down_m, (0,)),
                         (down_v, (0,)))
    down_other = swap(new_down, "xh")

    mix = [
        jnp.where(pick, term, 0).reshape(rings * 2 * slots, 4 * count)
        for term in split_three(lane_scale)
    ]
    mixed = dot_tn(jnp.concatenate(mix, axis=1), back).reshape(3, 4 * count, feature)
    mixed = mixed[0] + mixed[1] + mixed[2]
    theirs = mixed[2 * count:].astype(BF16)
    ours = swap(theirs, "xh").astype(F32)
    layer_out = (mixed[:count] + ours[:count]).astype(BF16)
    input_grad = (mixed[count:2 * count] + ours[count:]).astype(BF16)
    new_down = settle(flag, [new_down, down_other], layer_out)
    return layer_out, input_grad, new_gate_up[None], new_down


def solution(mesh):
    wide = Mesh(mesh.devices.reshape(2, 4, 8, 2, 2), ALL)
    token_spec = P(ALL, None)
    expert, share = ("xh", "y", "z"), ("xl", "core")
    up_spec = P(expert, None, share, None)
    down_spec = P(expert, share, None)
    return jax.shard_map(
        body,
        mesh=wide,
        in_specs=(token_spec, token_spec, token_spec, token_spec, P(), up_spec, down_spec, up_spec,
                  up_spec, down_spec, down_spec),
        out_specs=(token_spec, token_spec, up_spec, down_spec),
        check_vma=False,
    )
```

```python
import jax
import jax.numpy as jnp
from jax import lax
from jax.experimental import pallas as pl
from jax.experimental.pallas import tpu as pltpu
from jax.sharding import Mesh, PartitionSpec as P

BETA_ONE = 0.9
BETA_TWO = 0.95
STEP_RATE = 0.01
ADAM_EPS = 1e-08

F32 = jnp.float32
BF16 = jnp.bfloat16
CAP = 6
RINGS = ("y", "z")
ALL = ("xh", "y", "z", "xl", "core")


def swap(block, axis):
    return lax.ppermute(block, axis, [(0, 1), (1, 0)])


def after(value, *earlier):
    return lax.optimization_barrier((value, *earlier))[0]


def adam_update(weight, moment_one, moment_two, gradient):
    one_new = BETA_ONE * moment_one.astype(F32) + (1.0 - BETA_ONE) * gradient
    two_new = BETA_TWO * moment_two.astype(F32) + (1.0 - BETA_TWO) * gradient * gradient
    return (weight.astype(F32) - STEP_RATE * one_new / (jnp.sqrt(two_new) + ADAM_EPS)).astype(BF16)


def dot_nt(left, right):
    return lax.dot_general(left, right, (((1,), (1,)), ((), ())), preferred_element_type=F32)


def dot_nn(left, right):
    return lax.dot_general(left, right, (((1,), (0,)), ((), ())), preferred_element_type=F32)


def dot_tn(left, right):
    return lax.dot_general(left, right, (((0,), (0,)), ((), ())), preferred_element_type=F32)


CHUNK = 256
LANES = 512
VMEM_LIMIT = 56 * 1024 * 1024
META = 128


def pick_kernel(place_ref, g_ref, *outs):
    total = g_ref.shape[0]
    feature = outs[0].shape[1] // 2
    rows = outs[0].shape[0]
    meta = jnp.transpose(g_ref[:, 2 * feature:].astype(F32))
    names = meta[0:8]
    weights = meta[8:16] + meta[16:24] + meta[24:32]
    at = lax.broadcasted_iota(jnp.int32, (total, total), 0)
    to = lax.broadcasted_iota(jnp.int32, (total, total), 1)
    before = ((at < to) & ((at >> 5) == (to >> 5))).astype(BF16)
    row = lax.broadcasted_iota(jnp.int32, (rows, total), 0)
    source = (row * 43) >> 8
    number = (row - CAP * source).astype(F32)
    same = (lax.broadcasted_iota(jnp.int32, (rows, total), 1) >> 5) == source
    picks, scales = [], []
    for step in range(len(outs)):
        expert = place_ref[0] + 8 * ((place_ref[1] + step) & 3)
        hit = names == expert.astype(F32)
        used = jnp.sum(hit.astype(F32), axis=0, keepdims=True)
        weight = jnp.sum(jnp.where(hit, weights, 0.0), axis=0, keepdims=True)
        rank = jnp.sum(dot_nn(hit.astype(BF16), before), axis=0, keepdims=True)
        rank = jnp.where(used > 0, rank, -1.0)
        pick = same & (rank == number)
        picks.append(jnp.where(pick, 1.0, 0.0))
        scales.append(jnp.sum(jnp.where(pick, weight, 0.0), axis=1, keepdims=True))
    picks = jnp.concatenate(picks).astype(BF16)
    scales = jnp.concatenate(scales)
    for n in range(0, 2 * feature, LANES):
        found = dot_nn(picks, g_ref[:, n:n + LANES])
        if n >= feature:
            found = found * scales
        found = found.astype(BF16)
        for i, out in enumerate(outs):
            out[:, n:n + LANES] = found[i * rows:(i + 1) * rows]


def pick_step(place, gathered, steps):
    total, width = gathered.shape
    rows = total // 32 * CAP
    vmem_spec = pl.BlockSpec(memory_space=pltpu.VMEM)
    wide = (width - META) // 2
    return pl.pallas_call(
        pick_kernel,
        out_shape=(jax.ShapeDtypeStruct((rows, 2 * wide), BF16),) * steps,
        in_specs=[pl.BlockSpec(memory_space=pltpu.SMEM), vmem_spec],
        out_specs=(vmem_spec,) * steps,
        compiler_params=pltpu.CompilerParams(vmem_limit_bytes=VMEM_LIMIT),
        cost_estimate=pl.CostEstimate(
            flops=4 * steps * rows * total * wide,
            bytes_accessed=2 * (total * width + steps * rows * 2 * wide),
            transcendentals=0,
        ),
    )(place, gathered)


def rows_kernel(*refs):
    parts, order, weights, refs = refs[:8], refs[8], refs[9:17], refs[17:]
    (_m, back_ref, xd_out, act_out, g_gate, g_up, g_down,
     w_all, xd, acts, g_all, r_sem, w_sem, xd_sem, act_sem, g_sem) = refs
    share = weights[0].shape[1]
    width = 4 * share
    feature = back_ref.shape[1]
    size = parts[0].shape[0]
    arrivals = [
        pltpu.make_async_copy(
            part.at[:, pl.ds(side * feature, feature)], xd.at[side, pl.ds(i * size, size)], r_sem.at[2 * i + side]
        )
        for i, part in enumerate(parts)
        for side in range(2)
    ]
    for arrival in arrivals:
        arrival.start()
    loads = []
    for i, source in enumerate(weights):
        first, many = (2, 1) if i % 2 else (0, 2)
        loads.append(
            pltpu.make_async_copy(
                source, w_all.at[pl.ds(first, many), pl.ds(i // 2 * share, share)], w_sem.at[i]
            )
        )
    for load in loads:
        load.start()
    for arrival in arrivals:
        arrival.wait()
    xd_store = pltpu.make_async_copy(xd, xd_out, xd_sem)
    xd_store.start()

    done = 0
    for f in range(0, width, CHUNK):
        while done * share < f + CHUNK:
            loads[2 * done].wait()
            loads[2 * done + 1].wait()
            done += 1
        a = dot_nt(xd[0], w_all[0, f:f + CHUNK, :])
        u = dot_nt(xd[0], w_all[1, f:f + CHUNK, :])
        s = 1.0 / (1.0 + jnp.exp(-a))
        dh = dot_nt(xd[1], w_all[2, f:f + CHUNK, :])
        acts[2, :, f:f + CHUNK] = (a * s * u).astype(BF16)
        acts[0, :, f:f + CHUNK] = (dh * u * s * (1.0 + a * (1.0 - s))).astype(BF16)
        acts[1, :, f:f + CHUNK] = (dh * a * s).astype(BF16)
    act_store = pltpu.make_async_copy(acts.at[:, :, pl.ds(2 * share, 2 * share)], act_out, act_sem)
    act_store.start()

    stores = []
    for i, (side, target) in enumerate(zip((0, 0, 1), (g_gate, g_up, g_down))):
        for n in range(0, feature, LANES):
            g_all[i, :, n:n + LANES] = dot_tn(
                acts[i, :, :2 * share], xd[side, :, n:n + LANES]
            ).astype(BF16)
        stores.append(pltpu.make_async_copy(g_all.at[i], target, g_sem.at[i]))
        stores[i].start()

    for n in range(0, feature, LANES):
        o = dot_nn(acts[2], w_all[2, :, n:n + LANES]).astype(BF16)
        dx = (
            dot_nn(acts[0], w_all[0, :, n:n + LANES]) + dot_nn(acts[1], w_all[1, :, n:n + LANES])
        ).astype(BF16)
        back_ref[:, n:n + LANES] = dot_nn(order[...], jnp.concatenate([o, dx])).astype(BF16)
    xd_store.wait()
    act_store.wait()
    for store in stores:
        store.wait()


def rows_step(parts, order, weights, m_xl):
    total = order.shape[0]
    _, share, feature = weights[0][0].shape
    half = total // 2
    any_spec = pl.BlockSpec(memory_space=pl.ANY)
    vmem_spec = pl.BlockSpec(memory_space=pltpu.VMEM)
    return pl.pallas_call(
        rows_kernel,
        out_shape=(
            jax.ShapeDtypeStruct((total, feature), BF16),
            jax.ShapeDtypeStruct((2, half, feature), BF16),
            jax.ShapeDtypeStruct((3, half, 2 * share), BF16),
        ) + (jax.ShapeDtypeStruct((2 * share, feature), BF16),) * 3,
        in_specs=[any_spec] * 8 + [vmem_spec] + [any_spec] * 9,
        out_specs=(vmem_spec,) + (any_spec,) * 5,
        scratch_shapes=[
            pltpu.VMEM((3, 4 * share, feature), BF16),
            pltpu.VMEM((2, half, feature), BF16),
            pltpu.VMEM((3, half, 4 * share), BF16),
            pltpu.VMEM((3, 2 * share, feature), BF16),
            pltpu.SemaphoreType.DMA((16,)),
            pltpu.SemaphoreType.DMA((8,)),
            pltpu.SemaphoreType.DMA,
            pltpu.SemaphoreType.DMA,
            pltpu.SemaphoreType.DMA((3,)),
        ],
        compiler_params=pltpu.CompilerParams(vmem_limit_bytes=VMEM_LIMIT),
        cost_estimate=pl.CostEstimate(
            flops=half * feature * share,
            bytes_accessed=half * feature,
            transcendentals=0,
        ),
    )(*parts, order, *[array for pair in weights for array in pair], m_xl)


def grads_kernel(flag_ref, xd_ref, act_ref, core_gate, core_up, core_down, _mv, *outs):
    share = core_gate.shape[0] // 2
    moved = flag_ref[0] != 0
    for i, (side, core_ref) in enumerate(zip((0, 0, 1), (core_gate, core_up, core_down))):
        g = dot_tn(act_ref[i], xd_ref[side]) + core_ref[...].astype(F32)
        own = g[:share]
        other = g[share:]
        if i < 1:
            own, other = jnp.where(moved, other, own), jnp.where(moved, own, other)
        outs[i][...] = own.astype(BF16)
        outs[3 + i][...] = other.astype(BF16)


def grads_step(flag, xd, acts, core, mv_xl):
    _, half, feature = xd.shape
    share = core[0].shape[0] // 2
    out = jax.ShapeDtypeStruct((share, feature), BF16)
    return pl.pallas_call(
        grads_kernel,
        grid=(feature // LANES,),
        out_shape=(out,) * 6,
        in_specs=[
            pl.BlockSpec(memory_space=pltpu.SMEM),
            pl.BlockSpec((2, half, LANES), lambda n: (0, 0, n)),
            pl.BlockSpec(acts.shape, lambda n: (0, 0, 0)),
            *[pl.BlockSpec((2 * share, LANES), lambda n: (0, n))] * 3,
            pl.BlockSpec(memory_space=pl.ANY),
        ],
        out_specs=(pl.BlockSpec((share, LANES), lambda n: (0, n)),) * 6,
        compiler_params=pltpu.CompilerParams(vmem_limit_bytes=VMEM_LIMIT),
        cost_estimate=pl.CostEstimate(
            flops=12 * half * feature * share,
            bytes_accessed=2 * (2 * half * feature + 12 * share * feature),
            transcendentals=0,
        ),
    )(flag, xd, acts, *core, mv_xl)


def adam_kernel(flag_ref, keep_ref, recv_ref, *refs):
    moved = flag_ref[0] != 0
    out_ref = refs[-1]
    if len(refs) == 7:
        w, m, v = [
            jnp.where(moved, refs[i + 3][...].astype(F32), refs[i][...].astype(F32)) for i in range(3)
        ]
    else:
        w, m, v = [ref[...].astype(F32) for ref in refs[:3]]
    gradient = keep_ref[...].astype(F32) + recv_ref[...].astype(F32)
    out_ref[...] = adam_update(w, m, v, gradient)


def adam_step(flag, *arrays):
    rows, feature = arrays[0][0].shape[-2:]
    steps = 4

    def spec(lead):
        return pl.BlockSpec((None,) * len(lead) + (rows // steps, feature), lambda n: (*lead, n, 0))

    return pl.pallas_call(
        adam_kernel,
        grid=(steps,),
        out_shape=jax.ShapeDtypeStruct((rows, feature), BF16),
        in_specs=[pl.BlockSpec(memory_space=pltpu.SMEM)] + [spec(lead) for _, lead in arrays],
        out_specs=spec(()),
        compiler_params=pltpu.CompilerParams(vmem_limit_bytes=VMEM_LIMIT),
        cost_estimate=pl.CostEstimate(
            flops=20 * rows * feature,
            bytes_accessed=2 * (len(arrays) + 1) * rows * feature,
            transcendentals=rows * feature,
        ),
    )(flag, *[array for array, _ in arrays])


def settle_kernel(flag_ref, *refs):
    moved = flag_ref[0] != 0
    for i in range(refs[-1].shape[0]):
        refs[-1][i] = jnp.where(moved, refs[2 * i + 1][...], refs[2 * i][...])


def settle(flag, arrays, ready):
    rows, feature = arrays[0].shape
    count = len(arrays) // 2
    steps = 2
    block = pl.BlockSpec((rows // steps, feature), lambda n: (n, 0))
    return pl.pallas_call(
        settle_kernel,
        grid=(steps,),
        out_shape=jax.ShapeDtypeStruct((count, rows, feature), BF16),
        in_specs=[pl.BlockSpec(memory_space=pltpu.SMEM)] + [block] * len(arrays)
        + [pl.BlockSpec(memory_space=pl.ANY)],
        out_specs=pl.BlockSpec((count, rows // steps, feature), lambda n: (0, n, 0)),
        compiler_params=pltpu.CompilerParams(vmem_limit_bytes=VMEM_LIMIT),
        cost_estimate=pl.CostEstimate(
            flops=count * rows * feature, bytes_accessed=6 * count * rows * feature, transcendentals=0
        ),
    )(flag, *arrays, ready)


def split_three(value):
    high = value.astype(BF16)
    rest = value - high.astype(F32)
    middle = rest.astype(BF16)
    low = (rest - middle.astype(F32)).astype(BF16)
    return high, middle, low


def body(tokens, cotangent, routes, route_weights, matching, gate_up, down, gate_up_m, gate_up_v,
         down_m, down_v):
    half = lax.axis_index("xh")
    rings = lax.axis_size("y") * lax.axis_size("z")
    ring = lax.axis_index("y") * lax.axis_size("z") + lax.axis_index("z")
    self_index = half * rings + ring
    swapped = jnp.sum(jnp.where(jnp.arange(2 * rings) == self_index, matching, 0)) != self_index
    flag = swapped.astype(jnp.int32).reshape(1)
    count, feature = tokens.shape
    slots = 2 * CAP

    top = routes.shape[1]
    meta = jnp.concatenate([routes.astype(BF16), *split_three(route_weights)], axis=1)
    meta = jnp.pad(meta, ((0, 0), (0, META - 4 * top)))
    packed = jnp.concatenate([tokens, cotangent, meta], axis=1)
    packed_other = swap(packed, "xh")
    y_index = lax.axis_index("y")
    place = jnp.stack([half * rings + lax.axis_index("z"), y_index]).astype(jnp.int32)
    y_count = lax.axis_size("y")
    up_own, down_own = gate_up[0], down
    down_xl = swap(down_own, "xl")
    up_xl = swap(after(up_own, down_xl), "xl")
    parts_in, gathered = [], None
    for tile in (packed, packed_other):
        if gathered is not None:
            tile = after(tile, gathered)
        gathered = lax.all_gather(tile, "z", axis=0, tiled=True)
        gathered = after(gathered, *(parts_in[1:] or [down_xl]))
        picked = pick_step(place, gathered, y_count)
        parts_in.append(picked[0])
        for step in range(1, y_count):
            parts_in.append(
                lax.ppermute(picked[step], "y", [(i, (i + step) % y_count) for i in range(y_count)])
            )

    m_xl = swap(after(gate_up_m[0, :1], up_xl), "xl")
    v_xl = swap(after(gate_up_v[0, :1], m_xl), "xl")
    others_in = [m_xl, *parts_in[-3:]]
    weights = (
        (swap(up_own, "core"), swap(down_own, "core")),
        (swap(after(up_xl, *others_in), "core"), swap(after(down_xl, *others_in), "core")),
        (up_own, down_own),
        (up_xl, down_xl),
    )
    both = jnp.stack([meta, packed_other[:, 2 * feature:]]).astype(F32)
    both_routes = both[:, :, :top].astype(jnp.int32)
    both_weights = both[:, :, top:2 * top] + both[:, :, 2 * top:3 * top] + both[:, :, 3 * top:4 * top]
    ring_ids = jnp.arange(rings, dtype=jnp.int32)[:, None, None]
    hit = [both_routes[:, :, k] == half * rings + ring_ids for k in range(top)]
    used = sum(h.astype(jnp.int32) for h in hit)
    scale = sum(jnp.where(h, both_weights[:, :, k], 0.0) for k, h in enumerate(hit))
    before = (jnp.arange(count)[:, None] < jnp.arange(count)[None, :]).astype(BF16)
    earlier = jnp.dot(used.astype(BF16), before, preferred_element_type=F32).astype(jnp.int32)
    slot = earlier + CAP * jnp.arange(2, dtype=jnp.int32)[None, :, None]
    slot = jnp.where(used > 0, slot, -1)

    def on_lanes(value):
        return jnp.concatenate([value[:, 0], value[:, 0], value[:, 1], value[:, 1]], axis=1)[:, None]

    lane_kind = jnp.arange(4 * count, dtype=jnp.int32) // count % 2
    row = jnp.arange(2 * slots, dtype=jnp.int32)
    row_kind = row // slots
    row_slot = row % slots
    pick = (on_lanes(slot) == row_slot[:, None]) & (lane_kind == row_kind[:, None])
    lane_scale = jnp.where(lane_kind == 0, on_lanes(scale), 1.0)

    place_of = jnp.arange(rings * 2 * slots, dtype=jnp.int32)
    ring_of, within = place_of // (2 * slots), place_of % (2 * slots)
    slot_of = within % slots
    z_count = lax.axis_size("z")
    step_of = (y_index - ring_of // z_count) % y_count
    index = slot_of // CAP * y_count + step_of
    index = (index * z_count + ring_of % z_count) * CAP + slot_of % CAP + within // slots * (rings * slots)
    order = (index[:, None] == jnp.arange(rings * 2 * slots, dtype=jnp.int32)).astype(BF16)
    back_send, xd, acts, *g_pair = rows_step(parts_in, order, weights, m_xl)

    g_core = [swap(g, "core") for g in g_pair]
    back = lax.all_to_all(
        after(back_send, g_core[0]).reshape(rings, 2 * slots, feature), RINGS, split_axis=0, concat_axis=0, tiled=True
    ).reshape(-1, feature)
    parts = grads_step(flag, xd, acts, g_core, v_xl)
    others = [swap(parts[3], "xl"), swap(parts[4], "xl")]
    new_gate = adam_step(flag, (parts[0], ()), (others[0], ()), (gate_up, (0, 0)), (gate_up_m, (0, 0)),
                         (gate_up_v, (0, 0)), (up_xl, (0,)), (m_xl, (0,)), (v_xl, (0,)))
    others.append(swap(after(parts[5], new_gate), "xl"))
    gate_other = lax.ppermute(new_gate, ("xh", "xl"), [(0, 3), (3, 0), (1, 2), (2, 1)])
    new_up = adam_step(flag, (parts[1], ()), (others[1], ()), (gate_up, (0, 1)), (gate_up_m, (0, 1)),
                       (gate_up_v, (0, 1)))
    arrived = [new_gate, gate_other, new_up, swap(new_up, "xh")]
    new_gate_up = settle(flag, arrived, v_xl)
    new_down = adam_step(flag, (parts[2], ()), (others[2], ()), (down, (0,)), (down_m, (0,)),
                         (down_v, (0,)))
    down_other = swap(new_down, "xh")

    mix = [
        jnp.where(pick, term, 0).reshape(rings * 2 * slots, 4 * count)
        for term in split_three(lane_scale)
    ]
    mixed = dot_tn(jnp.concatenate(mix, axis=1), back).reshape(3, 4 * count, feature)
    mixed = mixed[0] + mixed[1] + mixed[2]
    theirs = mixed[2 * count:].astype(BF16)
    ours = swap(theirs, "xh").astype(F32)
    layer_out = (mixed[:count] + ours[:count]).astype(BF16)
    input_grad = (mixed[count:2 * count] + ours[count:]).astype(BF16)
    new_down = settle(flag, [new_down, down_other], layer_out)
    return layer_out, input_grad, new_gate_up[None], new_down


def solution(mesh):
    wide = Mesh(mesh.devices.reshape(2, 4, 8, 2, 2), ALL)
    token_spec = P(ALL, None)
    expert, share = ("xh", "y", "z"), ("xl", "core")
    up_spec = P(expert, None, share, None)
    down_spec = P(expert, share, None)
    return jax.shard_map(
        body,
        mesh=wide,
        in_specs=(token_spec, token_spec, token_spec, token_spec, P(), up_spec, down_spec, up_spec,
                  up_spec, down_spec, down_spec),
        out_specs=(token_spec, token_spec, up_spec, down_spec),
        check_vma=False,
    )
```

```python
import functools

import jax
import jax.numpy as jnp
from jax import lax
from jax.experimental import pallas as pl
from jax.experimental.pallas import tpu as pltpu
from jax.sharding import Mesh, PartitionSpec as P

BETA_ONE = 0.9
BETA_TWO = 0.95
STEP_RATE = 0.01
ADAM_EPS = 1e-08

F32 = jnp.float32
BF16 = jnp.bfloat16
CAP = 6
RINGS = ("y", "z")
ACROSS = [(0, 3), (3, 0), (1, 2), (2, 1)]
ALL = ("xh", "y", "z", "xl", "core")


def swap(block, axis):
    return lax.ppermute(block, axis, [(0, 1), (1, 0)])


def after(value, *earlier):
    return lax.optimization_barrier((value, *earlier))[0]


def adam_update(weight, moment_one, moment_two, gradient):
    one_new = BETA_ONE * moment_one.astype(F32) + (1.0 - BETA_ONE) * gradient
    two_new = BETA_TWO * moment_two.astype(F32) + (1.0 - BETA_TWO) * gradient * gradient
    return (weight.astype(F32) - STEP_RATE * one_new / (jnp.sqrt(two_new) + ADAM_EPS)).astype(BF16)


def dot_nt(left, right):
    return lax.dot_general(left, right, (((1,), (1,)), ((), ())), preferred_element_type=F32)


def dot_nn(left, right):
    return lax.dot_general(left, right, (((1,), (0,)), ((), ())), preferred_element_type=F32)


def dot_tn(left, right):
    return lax.dot_general(left, right, (((0,), (0,)), ((), ())), preferred_element_type=F32)


CHUNK = 256
LANES = 512
GROUP = 16
VMEM_LIMIT = 56 * 1024 * 1024


def mixed_order(size):
    to = lax.broadcasted_iota(jnp.int32, (size, size), 0)
    at = lax.broadcasted_iota(jnp.int32, (size, size), 1)
    part = to // (size // 2)
    row = to - part * (size // 2)
    return (at == (row // 4) * 8 + part * 4 + row % 4).astype(BF16)


def rows_kernel(rows_ref, w_own, w_xl, w_pair, _m, _v, back_ref, xd_out, act_out, g_gate, g_up, g_down,
                w_all, xd, mixed, acts, g_all, w_sem, xd_sem, act_sem, g_sem):
    share = w_own.shape[1]
    width = 4 * share
    rows = xd.shape[1]
    pairs = rows_ref.shape[0] // (3 * GROUP)
    plain = pairs * GROUP
    sources = (w_pair.at[0], w_pair.at[1], w_own, w_xl)
    loads = [
        pltpu.make_async_copy(src, w_all.at[:, pl.ds(i * share, share)], w_sem.at[i])
        for i, src in enumerate(sources)
    ]
    for load in loads:
        load.start()

    upper = lax.broadcasted_iota(jnp.int32, (GROUP, rows_ref.shape[1]), 0) < GROUP // 2

    def part(p, carry):
        base = pl.multiple_of(p * 3 * GROUP, GROUP)
        first = rows_ref[pl.ds(base, GROUP), :]
        last = rows_ref[pl.ds(base + 2 * GROUP, GROUP), :]
        to = pl.ds(pl.multiple_of(p * GROUP, GROUP), GROUP)
        xd[0, to, :] = jnp.where(upper, first, last)
        xd[1, to, :] = rows_ref[pl.ds(base + GROUP, GROUP), :]
        mixed[to, :] = jnp.where(upper, last, first)
        return carry

    lax.fori_loop(0, pairs, part, 0)
    order = mixed_order(plain)
    for n in range(0, rows_ref.shape[1], LANES):
        sorted_rows = dot_nn(order, mixed[:, n:n + LANES]).astype(BF16)
        xd[0, plain:, n:n + LANES] = sorted_rows[:plain // 2]
        xd[1, plain:, n:n + LANES] = sorted_rows[plain // 2:]
    xd_store = pltpu.make_async_copy(xd, xd_out, xd_sem)
    xd_store.start()

    done = 0
    for f in range(0, width, CHUNK):
        while done * share < f + CHUNK:
            loads[done].wait()
            done += 1
        a = dot_nt(xd[0], w_all[0, f:f + CHUNK, :])
        u = dot_nt(xd[0], w_all[1, f:f + CHUNK, :])
        s = 1.0 / (1.0 + jnp.exp(-a))
        dh = dot_nt(xd[1], w_all[2, f:f + CHUNK, :])
        acts[2, :, f:f + CHUNK] = (a * s * u).astype(BF16)
        acts[0, :, f:f + CHUNK] = (dh * u * s * (1.0 + a * (1.0 - s))).astype(BF16)
        acts[1, :, f:f + CHUNK] = (dh * a * s).astype(BF16)
    act_store = pltpu.make_async_copy(acts.at[:, :, pl.ds(2 * share, 2 * share)], act_out, act_sem)
    act_store.start()

    stores = []
    for i, (side, target) in enumerate(zip((0, 0, 1), (g_gate, g_up, g_down))):
        for n in range(0, rows_ref.shape[1], LANES):
            g_all[i, :, n:n + LANES] = dot_tn(
                acts[i, :, :2 * share], xd[side, :, n:n + LANES]
            ).astype(BF16)
        stores.append(pltpu.make_async_copy(g_all.at[i], target, g_sem.at[i]))
        stores[i].start()

    cut = lax.broadcasted_iota(jnp.int32, (GROUP, LANES), 0) < GROUP // 2
    for n in range(0, rows_ref.shape[1], LANES):
        o = dot_nn(acts[2], w_all[2, :, n:n + LANES]).astype(BF16)
        dx = (
            dot_nn(acts[0], w_all[0, :, n:n + LANES]) + dot_nn(acts[1], w_all[1, :, n:n + LANES])
        ).astype(BF16)
        blend = dot_tn(order, jnp.concatenate([o[plain:], dx[plain:]])).astype(BF16)
        for p in range(pairs):
            o_part = o[p * GROUP:(p + 1) * GROUP]
            m_part = blend[p * GROUP:(p + 1) * GROUP]
            base = p * 3 * GROUP
            back_ref[base:base + GROUP, n:n + LANES] = jnp.where(cut, o_part, m_part)
            back_ref[base + GROUP:base + 2 * GROUP, n:n + LANES] = dx[p * GROUP:(p + 1) * GROUP]
            back_ref[base + 2 * GROUP:base + 3 * GROUP, n:n + LANES] = jnp.where(cut, m_part, o_part)
    xd_store.wait()
    act_store.wait()
    for store in stores:
        store.wait()


def rows_step(rows, w_own, w_xl, w_pair, m_xl, v_xl):
    total, feature = rows.shape
    half = total // 2
    share = w_own.shape[1]
    any_spec = pl.BlockSpec(memory_space=pl.ANY)
    vmem_spec = pl.BlockSpec(memory_space=pltpu.VMEM)
    return pl.pallas_call(
        rows_kernel,
        out_shape=(
            jax.ShapeDtypeStruct(rows.shape, BF16),
            jax.ShapeDtypeStruct((2, half, feature), BF16),
            jax.ShapeDtypeStruct((3, half, 2 * share), BF16),
        ) + (jax.ShapeDtypeStruct((2 * share, feature), BF16),) * 3,
        in_specs=[vmem_spec] + [any_spec] * 5,
        out_specs=(vmem_spec,) + (any_spec,) * 5,
        scratch_shapes=[
            pltpu.VMEM((3, 4 * share, feature), BF16),
            pltpu.VMEM((2, half, feature), BF16),
            pltpu.VMEM((total // 3, feature), BF16),
            pltpu.VMEM((3, half, 4 * share), BF16),
            pltpu.VMEM((3, 2 * share, feature), BF16),
            pltpu.SemaphoreType.DMA((4,)),
            pltpu.SemaphoreType.DMA,
            pltpu.SemaphoreType.DMA,
            pltpu.SemaphoreType.DMA((3,)),
        ],
        compiler_params=pltpu.CompilerParams(vmem_limit_bytes=VMEM_LIMIT),
        cost_estimate=pl.CostEstimate(
            flops=half * feature * share,
            bytes_accessed=half * feature,
            transcendentals=0,
        ),
    )(rows, w_own, w_xl, w_pair, m_xl, v_xl)


def grads_kernel(exchange, flag_ref, rows_ref, act_ref, core_ref, *refs):
    keep_ref, send_ref = refs[-2:]
    share = core_ref.shape[0] // 2
    g = dot_tn(act_ref[...], rows_ref[...]) + core_ref[...].astype(F32)
    own, other = g[:share], g[share:]
    if exchange:
        moved = flag_ref[0] != 0
        own, other = jnp.where(moved, other, own), jnp.where(moved, own, other)
    keep_ref[...] = own.astype(BF16)
    send_ref[...] = other.astype(BF16)


def grads_step(exchange, flag, xd, side, acts, matrix, core, *ready):
    _, half, feature = xd.shape
    share = core.shape[0] // 2
    out = jax.ShapeDtypeStruct((share, feature), BF16)
    out_spec = pl.BlockSpec((share, LANES), lambda n: (0, n))
    return pl.pallas_call(
        functools.partial(grads_kernel, exchange),
        grid=(feature // LANES,),
        out_shape=(out,) * 2,
        in_specs=[
            pl.BlockSpec(memory_space=pltpu.SMEM),
            pl.BlockSpec((None, half, LANES), lambda n: (side, 0, n)),
            pl.BlockSpec((None, *acts.shape[1:]), lambda n: (matrix, 0, 0)),
            pl.BlockSpec((2 * share, LANES), lambda n: (0, n)),
        ] + [pl.BlockSpec(memory_space=pl.ANY)] * len(ready),
        out_specs=(out_spec,) * 2,
        compiler_params=pltpu.CompilerParams(vmem_limit_bytes=VMEM_LIMIT),
        cost_estimate=pl.CostEstimate(
            flops=4 * half * feature * share,
            bytes_accessed=2 * (half * feature + 4 * share * feature),
            transcendentals=0,
        ),
    )(flag, xd, acts, core, *ready)


def adam_kernel(flag_ref, keep_ref, recv_ref, *refs):
    moved = flag_ref[0] != 0
    out_ref = refs[-1]
    if len(refs) == 7:
        w, m, v = [
            jnp.where(moved, refs[i + 3][...].astype(F32), refs[i][...].astype(F32)) for i in range(3)
        ]
    else:
        w, m, v = [ref[...].astype(F32) for ref in refs[:3]]
    gradient = keep_ref[...].astype(F32) + recv_ref[...].astype(F32)
    out_ref[...] = adam_update(w, m, v, gradient)


def adam_step(flag, *arrays):
    rows, feature = arrays[0][0].shape[-2:]
    steps = 4

    def spec(lead):
        return pl.BlockSpec((None,) * len(lead) + (rows // steps, feature), lambda n: (*lead, n, 0))

    return pl.pallas_call(
        adam_kernel,
        grid=(steps,),
        out_shape=jax.ShapeDtypeStruct((rows, feature), BF16),
        in_specs=[pl.BlockSpec(memory_space=pltpu.SMEM)] + [spec(lead) for _, lead in arrays],
        out_specs=spec(()),
        compiler_params=pltpu.CompilerParams(vmem_limit_bytes=VMEM_LIMIT),
        cost_estimate=pl.CostEstimate(
            flops=20 * rows * feature,
            bytes_accessed=2 * (len(arrays) + 1) * rows * feature,
            transcendentals=rows * feature,
        ),
    )(flag, *[array for array, _ in arrays])


def settle_kernel(flag_ref, *refs):
    moved = flag_ref[0] != 0
    for i in range(refs[-1].shape[0]):
        refs[-1][i] = jnp.where(moved, refs[2 * i + 1][...], refs[2 * i][...])


def settle(flag, arrays, ready):
    rows, feature = arrays[0].shape
    count = len(arrays) // 2
    steps = 2
    block = pl.BlockSpec((rows // steps, feature), lambda n: (n, 0))
    return pl.pallas_call(
        settle_kernel,
        grid=(steps,),
        out_shape=jax.ShapeDtypeStruct((count, rows, feature), BF16),
        in_specs=[pl.BlockSpec(memory_space=pltpu.SMEM)] + [block] * len(arrays)
        + [pl.BlockSpec(memory_space=pl.ANY)],
        out_specs=pl.BlockSpec((count, rows // steps, feature), lambda n: (0, n, 0)),
        compiler_params=pltpu.CompilerParams(vmem_limit_bytes=VMEM_LIMIT),
        cost_estimate=pl.CostEstimate(
            flops=count * rows * feature, bytes_accessed=6 * count * rows * feature, transcendentals=0
        ),
    )(flag, *arrays, ready)


def split_three(value):
    high = value.astype(BF16)
    rest = value - high.astype(F32)
    middle = rest.astype(BF16)
    low = (rest - middle.astype(F32)).astype(BF16)
    return high, middle, low


def body(tokens, cotangent, routes, route_weights, matching, gate_up, down, gate_up_m, gate_up_v,
         down_m, down_v):
    half = lax.axis_index("xh")
    rings = lax.axis_size("y") * lax.axis_size("z")
    ring = lax.axis_index("y") * lax.axis_size("z") + lax.axis_index("z")
    self_index = half * rings + ring
    swapped = jnp.sum(jnp.where(jnp.arange(2 * rings) == self_index, matching, 0)) != self_index
    flag = swapped.astype(jnp.int32).reshape(1)
    count, feature = tokens.shape
    slots = 2 * CAP

    top = routes.shape[1]
    named = jnp.concatenate([routes.astype(F32), route_weights], axis=1)
    named_other = swap(named, "xh")
    tokens_other = swap(tokens, "xh")
    cotangent_other = swap(cotangent, "xh")
    source = jnp.concatenate([tokens, cotangent, tokens_other, cotangent_other])

    w_own = jnp.concatenate([gate_up[0], down])
    w_first = w_own
    w_xl = swap(w_first, "xl")
    w_pair = swap(jnp.stack([w_own, w_xl]), "core")

    both = jnp.stack([named, named_other])
    both_routes = both[:, :, :top].astype(jnp.int32)
    both_weights = both[:, :, top:]
    ring_ids = jnp.arange(rings, dtype=jnp.int32)[:, None, None]
    hit = [both_routes[:, :, k] == half * rings + ring_ids for k in range(top)]
    used = sum(h.astype(jnp.int32) for h in hit)
    scale = sum(jnp.where(h, both_weights[:, :, k], 0.0) for k, h in enumerate(hit))
    before = (jnp.arange(count)[:, None] < jnp.arange(count)[None, :]).astype(BF16)
    earlier = jnp.dot(used.astype(BF16), before, preferred_element_type=F32).astype(jnp.int32)
    slot = earlier + CAP * jnp.arange(2, dtype=jnp.int32)[None, :, None]
    slot = jnp.where(used > 0, slot, -1)

    def on_lanes(value):
        return jnp.concatenate([value[:, 0], value[:, 0], value[:, 1], value[:, 1]], axis=1)[:, None]

    lane_kind = jnp.arange(4 * count, dtype=jnp.int32) // count % 2
    row = jnp.arange(2 * slots, dtype=jnp.int32)
    row = jnp.where(ring % 2 == 0, row, jnp.where(row < 8, row + 16, jnp.where(row < 16, row, row - 16)))
    row_kind = (row >= 12).astype(jnp.int32)
    row_slot = jnp.where(row < 12, row, jnp.where(row < 16, row - 4, row - 16))
    pick = (on_lanes(slot) == row_slot[:, None]) & (lane_kind == row_kind[:, None])
    lane_scale = jnp.where(lane_kind == 0, on_lanes(scale), 1.0)
    row_scale = jnp.sum(jnp.where(pick, on_lanes(scale), 0.0), axis=2)
    factor = jnp.where(row_kind == 0, 1.0, row_scale).reshape(-1, 1)
    pick_b = pick.astype(BF16).reshape(rings * 2 * slots, 4 * count)
    send = (dot_nn(pick_b, source) * factor).astype(BF16).reshape(rings, 2 * slots, feature)

    m_xl = swap(after(gate_up_m[0, :1], send), "xl")
    v_xl = swap(after(gate_up_v[0, :1], send), "xl")

    recv = lax.all_to_all(send, RINGS, split_axis=0, concat_axis=0, tiled=True)
    back_send, xd, acts, *g_pair = rows_step(recv.reshape(-1, feature), w_own, w_xl, w_pair, m_xl, v_xl)

    g_core = [swap(g, "core") for g in g_pair]
    gate = grads_step(True, flag, xd, 0, acts, 0, g_core[0])
    up = grads_step(False, flag, xd, 0, acts, 1, g_core[1], gate[0])
    down_g = grads_step(False, flag, xd, 1, acts, 2, g_core[2], up[0])
    back = lax.all_to_all(
        after(back_send, g_core[0]).reshape(recv.shape), RINGS, split_axis=0, concat_axis=0, tiled=True
    ).reshape(-1, feature)
    parts = (gate[0], up[0], down_g[0], gate[1], up[1], down_g[1])
    others = [swap(parts[3], "xl"), swap(parts[4], "xl")]
    new_gate = adam_step(flag, (parts[0], ()), (others[0], ()), (gate_up, (0, 0)), (gate_up_m, (0, 0)),
                         (gate_up_v, (0, 0)), (w_xl, (0,)), (m_xl, (0,)), (v_xl, (0,)))
    others.append(swap(after(parts[5], new_gate), "xl"))
    gate_other = lax.ppermute(new_gate, ("xh", "xl"), ACROSS)
    new_up = adam_step(flag, (parts[1], ()), (others[1], ()), (gate_up, (0, 1)), (gate_up_m, (0, 1)),
                       (gate_up_v, (0, 1)))
    arrived = [new_gate, gate_other, new_up, swap(new_up, "xh")]
    new_gate_up = settle(flag, arrived, m_xl)
    new_down = adam_step(flag, (parts[2], ()), (others[2], ()), (down, (0,)), (down_m, (0,)),
                         (down_v, (0,)))
    down_other = swap(new_down, "xh")

    mix = [
        jnp.where(pick, term, 0).reshape(rings * 2 * slots, 4 * count)
        for term in split_three(lane_scale)
    ]
    mixed = dot_tn(jnp.concatenate(mix, axis=1), back).reshape(3, 4 * count, feature)
    mixed = mixed[0] + mixed[1] + mixed[2]
    theirs = mixed[2 * count:].astype(BF16)
    ours = swap(theirs, "xh").astype(F32)
    layer_out = (mixed[:count] + ours[:count]).astype(BF16)
    input_grad = (mixed[count:2 * count] + ours[count:]).astype(BF16)
    new_down = settle(flag, [new_down, down_other], layer_out)
    return layer_out, input_grad, new_gate_up[None], new_down


def solution(mesh):
    wide = Mesh(mesh.devices.reshape(2, 4, 8, 2, 2), ALL)
    token_spec = P(ALL, None)
    expert, share = ("xh", "y", "z"), ("xl", "core")
    up_spec = P(expert, None, share, None)
    down_spec = P(expert, share, None)
    return jax.shard_map(
        body,
        mesh=wide,
        in_specs=(token_spec, token_spec, token_spec, token_spec, P(), up_spec, down_spec, up_spec,
                  up_spec, down_spec, down_spec),
        out_specs=(token_spec, token_spec, up_spec, down_spec),
        check_vma=False,
    )
```

```python
import functools

import jax
import jax.numpy as jnp
from jax import lax
from jax.experimental import pallas as pl
from jax.experimental.pallas import tpu as pltpu
from jax.sharding import Mesh, PartitionSpec as P

BETA_ONE = 0.9
BETA_TWO = 0.95
STEP_RATE = 0.01
ADAM_EPS = 1e-08

F32 = jnp.float32
BF16 = jnp.bfloat16
CAP = 6
RINGS = ("y", "z")
ACROSS = [(0, 3), (3, 0), (1, 2), (2, 1)]
ALL = ("xh", "y", "z", "xl", "core")


def swap(block, axis):
    return lax.ppermute(block, axis, [(0, 1), (1, 0)])


def after(value, *earlier):
    return lax.optimization_barrier((value, *earlier))[0]


def adam_update(weight, moment_one, moment_two, gradient):
    one_new = BETA_ONE * moment_one.astype(F32) + (1.0 - BETA_ONE) * gradient
    two_new = BETA_TWO * moment_two.astype(F32) + (1.0 - BETA_TWO) * gradient * gradient
    return (weight.astype(F32) - STEP_RATE * one_new / (jnp.sqrt(two_new) + ADAM_EPS)).astype(BF16)


def dot_nt(left, right):
    return lax.dot_general(left, right, (((1,), (1,)), ((), ())), preferred_element_type=F32)


def dot_nn(left, right):
    return lax.dot_general(left, right, (((1,), (0,)), ((), ())), preferred_element_type=F32)


def dot_tn(left, right):
    return lax.dot_general(left, right, (((0,), (0,)), ((), ())), preferred_element_type=F32)


CHUNK = 256
LANES = 512
GROUP = 16
VMEM_LIMIT = 56 * 1024 * 1024


def mixed_order(size):
    to = lax.broadcasted_iota(jnp.int32, (size, size), 0)
    at = lax.broadcasted_iota(jnp.int32, (size, size), 1)
    part = to // (size // 2)
    row = to - part * (size // 2)
    return (at == (row // 4) * 8 + part * 4 + row % 4).astype(BF16)


def rows_kernel(rows_ref, w_own, w_xl, w_pair, _m, _v, back_ref, xd_out, act_out, g_gate, g_up, g_down,
                w_all, xd, mixed, acts, g_all, w_sem, xd_sem, act_sem, g_sem):
    share = w_own.shape[1]
    width = 4 * share
    rows = xd.shape[1]
    pairs = rows_ref.shape[0] // (3 * GROUP)
    plain = pairs * GROUP
    sources = (w_pair.at[0], w_pair.at[1], w_own, w_xl)
    loads = [
        pltpu.make_async_copy(src, w_all.at[:, pl.ds(i * share, share)], w_sem.at[i])
        for i, src in enumerate(sources)
    ]
    for load in loads:
        load.start()

    upper = lax.broadcasted_iota(jnp.int32, (GROUP, rows_ref.shape[1]), 0) < GROUP // 2

    def part(p, carry):
        base = pl.multiple_of(p * 3 * GROUP, GROUP)
        first = rows_ref[pl.ds(base, GROUP), :]
        last = rows_ref[pl.ds(base + 2 * GROUP, GROUP), :]
        to = pl.ds(pl.multiple_of(p * GROUP, GROUP), GROUP)
        xd[0, to, :] = jnp.where(upper, first, last)
        xd[1, to, :] = rows_ref[pl.ds(base + GROUP, GROUP), :]
        mixed[to, :] = jnp.where(upper, last, first)
        return carry

    lax.fori_loop(0, pairs, part, 0)
    order = mixed_order(plain)
    for n in range(0, rows_ref.shape[1], LANES):
        sorted_rows = dot_nn(order, mixed[:, n:n + LANES]).astype(BF16)
        xd[0, plain:, n:n + LANES] = sorted_rows[:plain // 2]
        xd[1, plain:, n:n + LANES] = sorted_rows[plain // 2:]
    xd_store = pltpu.make_async_copy(xd, xd_out, xd_sem)
    xd_store.start()

    done = 0
    for f in range(0, width, CHUNK):
        while done * share < f + CHUNK:
            loads[done].wait()
            done += 1
        a = dot_nt(xd[0], w_all[0, f:f + CHUNK, :])
        u = dot_nt(xd[0], w_all[1, f:f + CHUNK, :])
        s = 1.0 / (1.0 + jnp.exp(-a))
        dh = dot_nt(xd[1], w_all[2, f:f + CHUNK, :])
        acts[2, :, f:f + CHUNK] = (a * s * u).astype(BF16)
        acts[0, :, f:f + CHUNK] = (dh * u * s * (1.0 + a * (1.0 - s))).astype(BF16)
        acts[1, :, f:f + CHUNK] = (dh * a * s).astype(BF16)
    act_store = pltpu.make_async_copy(acts.at[:, :, pl.ds(2 * share, 2 * share)], act_out, act_sem)
    act_store.start()

    stores = []
    for i, (side, target) in enumerate(zip((0, 0, 1), (g_gate, g_up, g_down))):
        for n in range(0, rows_ref.shape[1], LANES):
            g_all[i, :, n:n + LANES] = dot_tn(
                acts[i, :, :2 * share], xd[side, :, n:n + LANES]
            ).astype(BF16)
        stores.append(pltpu.make_async_copy(g_all.at[i], target, g_sem.at[i]))
        stores[i].start()

    cut = lax.broadcasted_iota(jnp.int32, (GROUP, LANES), 0) < GROUP // 2
    for n in range(0, rows_ref.shape[1], LANES):
        o = dot_nn(acts[2], w_all[2, :, n:n + LANES]).astype(BF16)
        dx = (
            dot_nn(acts[0], w_all[0, :, n:n + LANES]) + dot_nn(acts[1], w_all[1, :, n:n + LANES])
        ).astype(BF16)
        blend = dot_tn(order, jnp.concatenate([o[plain:], dx[plain:]])).astype(BF16)
        for p in range(pairs):
            o_part = o[p * GROUP:(p + 1) * GROUP]
            m_part = blend[p * GROUP:(p + 1) * GROUP]
            base = p * 3 * GROUP
            back_ref[base:base + GROUP, n:n + LANES] = jnp.where(cut, o_part, m_part)
            back_ref[base + GROUP:base + 2 * GROUP, n:n + LANES] = dx[p * GROUP:(p + 1) * GROUP]
            back_ref[base + 2 * GROUP:base + 3 * GROUP, n:n + LANES] = jnp.where(cut, m_part, o_part)
    xd_store.wait()
    act_store.wait()
    for store in stores:
        store.wait()


def rows_step(rows, w_own, w_xl, w_pair, m_xl, v_xl):
    total, feature = rows.shape
    half = total // 2
    share = w_own.shape[1]
    any_spec = pl.BlockSpec(memory_space=pl.ANY)
    vmem_spec = pl.BlockSpec(memory_space=pltpu.VMEM)
    return pl.pallas_call(
        rows_kernel,
        out_shape=(
            jax.ShapeDtypeStruct(rows.shape, BF16),
            jax.ShapeDtypeStruct((2, half, feature), BF16),
            jax.ShapeDtypeStruct((3, half, 2 * share), BF16),
        ) + (jax.ShapeDtypeStruct((2 * share, feature), BF16),) * 3,
        in_specs=[vmem_spec] + [any_spec] * 5,
        out_specs=(vmem_spec,) + (any_spec,) * 5,
        scratch_shapes=[
            pltpu.VMEM((3, 4 * share, feature), BF16),
            pltpu.VMEM((2, half, feature), BF16),
            pltpu.VMEM((total // 3, feature), BF16),
            pltpu.VMEM((3, half, 4 * share), BF16),
            pltpu.VMEM((3, 2 * share, feature), BF16),
            pltpu.SemaphoreType.DMA((4,)),
            pltpu.SemaphoreType.DMA,
            pltpu.SemaphoreType.DMA,
            pltpu.SemaphoreType.DMA((3,)),
        ],
        compiler_params=pltpu.CompilerParams(vmem_limit_bytes=VMEM_LIMIT),
        cost_estimate=pl.CostEstimate(
            flops=half * feature * share,
            bytes_accessed=half * feature,
            transcendentals=0,
        ),
    )(rows, w_own, w_xl, w_pair, m_xl, v_xl)


def grads_kernel(exchange, flag_ref, rows_ref, act_ref, core_ref, *refs):
    keep_ref, send_ref = refs[-2:]
    share = core_ref.shape[0] // 2
    g = dot_tn(act_ref[...], rows_ref[...]) + core_ref[...].astype(F32)
    own, other = g[:share], g[share:]
    if exchange:
        moved = flag_ref[0] != 0
        own, other = jnp.where(moved, other, own), jnp.where(moved, own, other)
    keep_ref[...] = own.astype(BF16)
    send_ref[...] = other.astype(BF16)


def grads_step(exchange, flag, xd, side, acts, matrix, core, *ready):
    _, half, feature = xd.shape
    share = core.shape[0] // 2
    out = jax.ShapeDtypeStruct((share, feature), BF16)
    out_spec = pl.BlockSpec((share, LANES), lambda n: (0, n))
    return pl.pallas_call(
        functools.partial(grads_kernel, exchange),
        grid=(feature // LANES,),
        out_shape=(out,) * 2,
        in_specs=[
            pl.BlockSpec(memory_space=pltpu.SMEM),
            pl.BlockSpec((None, half, LANES), lambda n: (side, 0, n)),
            pl.BlockSpec((None, *acts.shape[1:]), lambda n: (matrix, 0, 0)),
            pl.BlockSpec((2 * share, LANES), lambda n: (0, n)),
        ] + [pl.BlockSpec(memory_space=pl.ANY)] * len(ready),
        out_specs=(out_spec,) * 2,
        compiler_params=pltpu.CompilerParams(vmem_limit_bytes=VMEM_LIMIT),
        cost_estimate=pl.CostEstimate(
            flops=4 * half * feature * share,
            bytes_accessed=2 * (half * feature + 4 * share * feature),
            transcendentals=0,
        ),
    )(flag, xd, acts, core, *ready)


def adam_kernel(flag_ref, keep_ref, recv_ref, *refs):
    moved = flag_ref[0] != 0
    out_ref = refs[-1]
    if len(refs) == 7:
        w, m, v = [
            jnp.where(moved, refs[i + 3][...].astype(F32), refs[i][...].astype(F32)) for i in range(3)
        ]
    else:
        w, m, v = [ref[...].astype(F32) for ref in refs[:3]]
    gradient = keep_ref[...].astype(F32) + recv_ref[...].astype(F32)
    out_ref[...] = adam_update(w, m, v, gradient)


def adam_step(flag, *arrays):
    rows, feature = arrays[0][0].shape[-2:]
    steps = 4

    def spec(lead):
        return pl.BlockSpec((None,) * len(lead) + (rows // steps, feature), lambda n: (*lead, n, 0))

    return pl.pallas_call(
        adam_kernel,
        grid=(steps,),
        out_shape=jax.ShapeDtypeStruct((rows, feature), BF16),
        in_specs=[pl.BlockSpec(memory_space=pltpu.SMEM)] + [spec(lead) for _, lead in arrays],
        out_specs=spec(()),
        compiler_params=pltpu.CompilerParams(vmem_limit_bytes=VMEM_LIMIT),
        cost_estimate=pl.CostEstimate(
            flops=20 * rows * feature,
            bytes_accessed=2 * (len(arrays) + 1) * rows * feature,
            transcendentals=rows * feature,
        ),
    )(flag, *[array for array, _ in arrays])


def settle_kernel(flag_ref, *refs):
    moved = flag_ref[0] != 0
    for i in range(refs[-1].shape[0]):
        refs[-1][i] = jnp.where(moved, refs[2 * i + 1][...], refs[2 * i][...])


def settle(flag, arrays, ready):
    rows, feature = arrays[0].shape
    count = len(arrays) // 2
    steps = 2
    block = pl.BlockSpec((rows // steps, feature), lambda n: (n, 0))
    return pl.pallas_call(
        settle_kernel,
        grid=(steps,),
        out_shape=jax.ShapeDtypeStruct((count, rows, feature), BF16),
        in_specs=[pl.BlockSpec(memory_space=pltpu.SMEM)] + [block] * len(arrays)
        + [pl.BlockSpec(memory_space=pl.ANY)],
        out_specs=pl.BlockSpec((count, rows // steps, feature), lambda n: (0, n, 0)),
        compiler_params=pltpu.CompilerParams(vmem_limit_bytes=VMEM_LIMIT),
        cost_estimate=pl.CostEstimate(
            flops=count * rows * feature, bytes_accessed=6 * count * rows * feature, transcendentals=0
        ),
    )(flag, *arrays, ready)


def split_three(value):
    high = value.astype(BF16)
    rest = value - high.astype(F32)
    middle = rest.astype(BF16)
    low = (rest - middle.astype(F32)).astype(BF16)
    return high, middle, low


def body(tokens, cotangent, routes, route_weights, matching, gate_up, down, gate_up_m, gate_up_v,
         down_m, down_v):
    half = lax.axis_index("xh")
    rings = lax.axis_size("y") * lax.axis_size("z")
    ring = lax.axis_index("y") * lax.axis_size("z") + lax.axis_index("z")
    self_index = half * rings + ring
    swapped = jnp.sum(jnp.where(jnp.arange(2 * rings) == self_index, matching, 0)) != self_index
    flag = swapped.astype(jnp.int32).reshape(1)
    count, feature = tokens.shape
    slots = 2 * CAP

    top = routes.shape[1]
    named = jnp.concatenate([routes.astype(F32), route_weights], axis=1)
    named_other = swap(named, "xh")
    tokens_other = swap(tokens, "xh")
    cotangent_other = swap(cotangent, "xh")
    source = jnp.concatenate([tokens, cotangent, tokens_other, cotangent_other])

    w_own = jnp.concatenate([gate_up[0], down])
    w_first = w_own
    w_xl = swap(w_first, "xl")

    both = jnp.stack([named, named_other])
    both_routes = both[:, :, :top].astype(jnp.int32)
    both_weights = both[:, :, top:]
    ring_ids = jnp.arange(rings, dtype=jnp.int32)[:, None, None]
    hit = [both_routes[:, :, k] == half * rings + ring_ids for k in range(top)]
    used = sum(h.astype(jnp.int32) for h in hit)
    scale = sum(jnp.where(h, both_weights[:, :, k], 0.0) for k, h in enumerate(hit))
    before = (jnp.arange(count)[:, None] < jnp.arange(count)[None, :]).astype(BF16)
    earlier = jnp.dot(used.astype(BF16), before, preferred_element_type=F32).astype(jnp.int32)
    slot = earlier + CAP * jnp.arange(2, dtype=jnp.int32)[None, :, None]
    slot = jnp.where(used > 0, slot, -1)

    def on_lanes(value):
        return jnp.concatenate([value[:, 0], value[:, 0], value[:, 1], value[:, 1]], axis=1)[:, None]

    lane_kind = jnp.arange(4 * count, dtype=jnp.int32) // count % 2
    row = jnp.arange(2 * slots, dtype=jnp.int32)
    row = jnp.where(ring % 2 == 0, row, jnp.where(row < 8, row + 16, jnp.where(row < 16, row, row - 16)))
    row_kind = (row >= 12).astype(jnp.int32)
    row_slot = jnp.where(row < 12, row, jnp.where(row < 16, row - 4, row - 16))
    pick = (on_lanes(slot) == row_slot[:, None]) & (lane_kind == row_kind[:, None])
    lane_scale = jnp.where(lane_kind == 0, on_lanes(scale), 1.0)
    row_scale = jnp.sum(jnp.where(pick, on_lanes(scale), 0.0), axis=2)
    factor = jnp.where(row_kind == 0, 1.0, row_scale).reshape(-1, 1)
    pick_b = pick.astype(BF16).reshape(rings * 2 * slots, 4 * count)
    send = (dot_nn(pick_b, source) * factor).astype(BF16).reshape(rings, 2 * slots, feature)

    m_xl = swap(after(gate_up_m[0, :1], send), "xl")
    v_xl = swap(after(gate_up_v[0, :1], send), "xl")
    w_pair = swap(jnp.stack([w_own, after(w_xl, m_xl)]), "core")

    recv = lax.all_to_all(send, RINGS, split_axis=0, concat_axis=0, tiled=True)
    back_send, xd, acts, *g_pair = rows_step(recv.reshape(-1, feature), w_own, w_xl, w_pair, m_xl, v_xl)

    g_core = [swap(g, "core") for g in g_pair]
    gate = grads_step(True, flag, xd, 0, acts, 0, g_core[0])
    up = grads_step(False, flag, xd, 0, acts, 1, g_core[1], gate[0])
    down_g = grads_step(False, flag, xd, 1, acts, 2, g_core[2], up[0])
    back = lax.all_to_all(
        after(back_send, gate[0]).reshape(recv.shape), RINGS, split_axis=0, concat_axis=0, tiled=True
    ).reshape(-1, feature)
    parts = (gate[0], up[0], down_g[0], gate[1], up[1], down_g[1])
    others = [swap(parts[3], "xl"), swap(parts[4], "xl")]
    new_gate = adam_step(flag, (parts[0], ()), (others[0], ()), (gate_up, (0, 0)), (gate_up_m, (0, 0)),
                         (gate_up_v, (0, 0)), (w_xl, (0,)), (m_xl, (0,)), (v_xl, (0,)))
    others.append(swap(after(parts[5], new_gate), "xl"))
    gate_other = lax.ppermute(new_gate, ("xh", "xl"), ACROSS)
    new_up = adam_step(flag, (parts[1], ()), (others[1], ()), (gate_up, (0, 1)), (gate_up_m, (0, 1)),
                       (gate_up_v, (0, 1)))
    arrived = [new_gate, gate_other, new_up, swap(new_up, "xh")]
    new_gate_up = settle(flag, arrived, m_xl)
    new_down = adam_step(flag, (parts[2], ()), (others[2], ()), (down, (0,)), (down_m, (0,)),
                         (down_v, (0,)))
    down_other = swap(new_down, "xh")

    mix = [
        jnp.where(pick, term, 0).reshape(rings * 2 * slots, 4 * count)
        for term in split_three(lane_scale)
    ]
    mixed = dot_tn(jnp.concatenate(mix, axis=1), back).reshape(3, 4 * count, feature)
    mixed = mixed[0] + mixed[1] + mixed[2]
    theirs = mixed[2 * count:].astype(BF16)
    ours = swap(theirs, "xh").astype(F32)
    layer_out = (mixed[:count] + ours[:count]).astype(BF16)
    input_grad = (mixed[count:2 * count] + ours[count:]).astype(BF16)
    new_down = settle(flag, [new_down, down_other], layer_out)
    return layer_out, input_grad, new_gate_up[None], new_down


def solution(mesh):
    wide = Mesh(mesh.devices.reshape(2, 4, 8, 2, 2), ALL)
    token_spec = P(ALL, None)
    expert, share = ("xh", "y", "z"), ("xl", "core")
    up_spec = P(expert, None, share, None)
    down_spec = P(expert, share, None)
    return jax.shard_map(
        body,
        mesh=wide,
        in_specs=(token_spec, token_spec, token_spec, token_spec, P(), up_spec, down_spec, up_spec,
                  up_spec, down_spec, down_spec),
        out_specs=(token_spec, token_spec, up_spec, down_spec),
        check_vma=False,
    )
```

```python
import functools

import jax
import jax.numpy as jnp
from jax import lax
from jax.experimental import pallas as pl
from jax.experimental.pallas import tpu as pltpu
from jax.sharding import Mesh, PartitionSpec as P

BETA_ONE = 0.9
BETA_TWO = 0.95
STEP_RATE = 0.01
ADAM_EPS = 1e-08

F32 = jnp.float32
BF16 = jnp.bfloat16
CAP = 6
RINGS = ("y", "z")
ACROSS = [(0, 3), (3, 0), (1, 2), (2, 1)]
ALL = ("xh", "y", "z", "xl", "core")


def swap(block, axis):
    return lax.ppermute(block, axis, [(0, 1), (1, 0)])


def after(value, *earlier):
    return lax.optimization_barrier((value, *earlier))[0]


def adam_update(weight, moment_one, moment_two, gradient):
    one_new = BETA_ONE * moment_one.astype(F32) + (1.0 - BETA_ONE) * gradient
    two_new = BETA_TWO * moment_two.astype(F32) + (1.0 - BETA_TWO) * gradient * gradient
    return (weight.astype(F32) - STEP_RATE * one_new / (jnp.sqrt(two_new) + ADAM_EPS)).astype(BF16)


def dot_nt(left, right):
    return lax.dot_general(left, right, (((1,), (1,)), ((), ())), preferred_element_type=F32)


def dot_nn(left, right):
    return lax.dot_general(left, right, (((1,), (0,)), ((), ())), preferred_element_type=F32)


def dot_tn(left, right):
    return lax.dot_general(left, right, (((0,), (0,)), ((), ())), preferred_element_type=F32)


CHUNK = 256
LANES = 512
GROUP = 16
VMEM_LIMIT = 56 * 1024 * 1024


def mixed_order(size):
    to = lax.broadcasted_iota(jnp.int32, (size, size), 0)
    at = lax.broadcasted_iota(jnp.int32, (size, size), 1)
    part = to // (size // 2)
    row = to - part * (size // 2)
    return (at == (row // 4) * 8 + part * 4 + row % 4).astype(BF16)


def rows_kernel(rows_ref, w_own, w_xl, w_pair, _mv, back_ref, xd_out, act_out, g_gate, g_up, g_down,
                w_all, xd, mixed, acts, g_all, w_sem, xd_sem, act_sem, g_sem):
    share = w_own.shape[1]
    width = 4 * share
    rows = xd.shape[1]
    pairs = rows_ref.shape[0] // (3 * GROUP)
    plain = pairs * GROUP
    sources = (w_pair.at[0], w_pair.at[1], w_own, w_xl)
    loads = [
        pltpu.make_async_copy(src, w_all.at[:, pl.ds(i * share, share)], w_sem.at[i])
        for i, src in enumerate(sources)
    ]
    for load in loads:
        load.start()

    upper = lax.broadcasted_iota(jnp.int32, (GROUP, rows_ref.shape[1]), 0) < GROUP // 2

    def part(p, carry):
        base = pl.multiple_of(p * 3 * GROUP, GROUP)
        first = rows_ref[pl.ds(base, GROUP), :]
        last = rows_ref[pl.ds(base + 2 * GROUP, GROUP), :]
        to = pl.ds(pl.multiple_of(p * GROUP, GROUP), GROUP)
        xd[0, to, :] = jnp.where(upper, first, last)
        xd[1, to, :] = rows_ref[pl.ds(base + GROUP, GROUP), :]
        mixed[to, :] = jnp.where(upper, last, first)
        return carry

    lax.fori_loop(0, pairs, part, 0)
    order = mixed_order(plain)
    for n in range(0, rows_ref.shape[1], LANES):
        sorted_rows = dot_nn(order, mixed[:, n:n + LANES]).astype(BF16)
        xd[0, plain:, n:n + LANES] = sorted_rows[:plain // 2]
        xd[1, plain:, n:n + LANES] = sorted_rows[plain // 2:]
    xd_store = pltpu.make_async_copy(xd, xd_out, xd_sem)
    xd_store.start()

    done = 0
    for f in range(0, width, CHUNK):
        while done * share < f + CHUNK:
            loads[done].wait()
            done += 1
        a = dot_nt(xd[0], w_all[0, f:f + CHUNK, :])
        u = dot_nt(xd[0], w_all[1, f:f + CHUNK, :])
        s = 1.0 / (1.0 + jnp.exp(-a))
        dh = dot_nt(xd[1], w_all[2, f:f + CHUNK, :])
        acts[2, :, f:f + CHUNK] = (a * s * u).astype(BF16)
        acts[0, :, f:f + CHUNK] = (dh * u * s * (1.0 + a * (1.0 - s))).astype(BF16)
        acts[1, :, f:f + CHUNK] = (dh * a * s).astype(BF16)
    act_store = pltpu.make_async_copy(acts.at[:, :, pl.ds(2 * share, 2 * share)], act_out, act_sem)
    act_store.start()

    stores = []
    for i, (side, target) in enumerate(zip((0, 0, 1), (g_gate, g_up, g_down))):
        for n in range(0, rows_ref.shape[1], LANES):
            g_all[i, :, n:n + LANES] = dot_tn(
                acts[i, :, :2 * share], xd[side, :, n:n + LANES]
            ).astype(BF16)
        stores.append(pltpu.make_async_copy(g_all.at[i], target, g_sem.at[i]))
        stores[i].start()

    cut = lax.broadcasted_iota(jnp.int32, (GROUP, LANES), 0) < GROUP // 2
    for n in range(0, rows_ref.shape[1], LANES):
        o = dot_nn(acts[2], w_all[2, :, n:n + LANES]).astype(BF16)
        dx = (
            dot_nn(acts[0], w_all[0, :, n:n + LANES]) + dot_nn(acts[1], w_all[1, :, n:n + LANES])
        ).astype(BF16)
        blend = dot_tn(order, jnp.concatenate([o[plain:], dx[plain:]])).astype(BF16)
        for p in range(pairs):
            o_part = o[p * GROUP:(p + 1) * GROUP]
            m_part = blend[p * GROUP:(p + 1) * GROUP]
            base = p * 3 * GROUP
            back_ref[base:base + GROUP, n:n + LANES] = jnp.where(cut, o_part, m_part)
            back_ref[base + GROUP:base + 2 * GROUP, n:n + LANES] = dx[p * GROUP:(p + 1) * GROUP]
            back_ref[base + 2 * GROUP:base + 3 * GROUP, n:n + LANES] = jnp.where(cut, m_part, o_part)
    xd_store.wait()
    act_store.wait()
    for store in stores:
        store.wait()


def rows_step(rows, w_own, w_xl, w_pair, mv_xl):
    total, feature = rows.shape
    half = total // 2
    share = w_own.shape[1]
    any_spec = pl.BlockSpec(memory_space=pl.ANY)
    vmem_spec = pl.BlockSpec(memory_space=pltpu.VMEM)
    return pl.pallas_call(
        rows_kernel,
        out_shape=(
            jax.ShapeDtypeStruct(rows.shape, BF16),
            jax.ShapeDtypeStruct((2, half, feature), BF16),
            jax.ShapeDtypeStruct((3, half, 2 * share), BF16),
        ) + (jax.ShapeDtypeStruct((2 * share, feature), BF16),) * 3,
        in_specs=[vmem_spec] + [any_spec] * 4,
        out_specs=(vmem_spec,) + (any_spec,) * 5,
        scratch_shapes=[
            pltpu.VMEM((3, 4 * share, feature), BF16),
            pltpu.VMEM((2, half, feature), BF16),
            pltpu.VMEM((total // 3, feature), BF16),
            pltpu.VMEM((3, half, 4 * share), BF16),
            pltpu.VMEM((3, 2 * share, feature), BF16),
            pltpu.SemaphoreType.DMA((4,)),
            pltpu.SemaphoreType.DMA,
            pltpu.SemaphoreType.DMA,
            pltpu.SemaphoreType.DMA((3,)),
        ],
        compiler_params=pltpu.CompilerParams(vmem_limit_bytes=VMEM_LIMIT),
        cost_estimate=pl.CostEstimate(
            flops=half * feature * share,
            bytes_accessed=half * feature,
            transcendentals=0,
        ),
    )(rows, w_own, w_xl, w_pair, mv_xl)


def grads_kernel(exchange, flag_ref, rows_ref, act_ref, core_ref, *refs):
    keep_ref, send_ref = refs[-2:]
    share = core_ref.shape[0] // 2
    g = dot_tn(act_ref[...], rows_ref[...]) + core_ref[...].astype(F32)
    own, other = g[:share], g[share:]
    if exchange:
        moved = flag_ref[0] != 0
        own, other = jnp.where(moved, other, own), jnp.where(moved, own, other)
    keep_ref[...] = own.astype(BF16)
    send_ref[...] = other.astype(BF16)


def grads_step(exchange, flag, xd, side, acts, matrix, core, *ready):
    _, half, feature = xd.shape
    share = core.shape[0] // 2
    out = jax.ShapeDtypeStruct((share, feature), BF16)
    out_spec = pl.BlockSpec((share, LANES), lambda n: (0, n))
    return pl.pallas_call(
        functools.partial(grads_kernel, exchange),
        grid=(feature // LANES,),
        out_shape=(out,) * 2,
        in_specs=[
            pl.BlockSpec(memory_space=pltpu.SMEM),
            pl.BlockSpec((None, half, LANES), lambda n: (side, 0, n)),
            pl.BlockSpec((None, *acts.shape[1:]), lambda n: (matrix, 0, 0)),
            pl.BlockSpec((2 * share, LANES), lambda n: (0, n)),
        ] + [pl.BlockSpec(memory_space=pl.ANY)] * len(ready),
        out_specs=(out_spec,) * 2,
        compiler_params=pltpu.CompilerParams(vmem_limit_bytes=VMEM_LIMIT),
        cost_estimate=pl.CostEstimate(
            flops=4 * half * feature * share,
            bytes_accessed=2 * (half * feature + 4 * share * feature),
            transcendentals=0,
        ),
    )(flag, xd, acts, core, *ready)


def adam_kernel(flag_ref, keep_ref, recv_ref, *refs):
    moved = flag_ref[0] != 0
    out_ref = refs[-1]
    if len(refs) == 7:
        w, m, v = [
            jnp.where(moved, refs[i + 3][...].astype(F32), refs[i][...].astype(F32)) for i in range(3)
        ]
    else:
        w, m, v = [ref[...].astype(F32) for ref in refs[:3]]
    gradient = keep_ref[...].astype(F32) + recv_ref[...].astype(F32)
    out_ref[...] = adam_update(w, m, v, gradient)


def adam_step(flag, *arrays):
    rows, feature = arrays[0][0].shape[-2:]
    steps = 4

    def spec(lead):
        return pl.BlockSpec((None,) * len(lead) + (rows // steps, feature), lambda n: (*lead, n, 0))

    return pl.pallas_call(
        adam_kernel,
        grid=(steps,),
        out_shape=jax.ShapeDtypeStruct((rows, feature), BF16),
        in_specs=[pl.BlockSpec(memory_space=pltpu.SMEM)] + [spec(lead) for _, lead in arrays],
        out_specs=spec(()),
        compiler_params=pltpu.CompilerParams(vmem_limit_bytes=VMEM_LIMIT),
        cost_estimate=pl.CostEstimate(
            flops=20 * rows * feature,
            bytes_accessed=2 * (len(arrays) + 1) * rows * feature,
            transcendentals=rows * feature,
        ),
    )(flag, *[array for array, _ in arrays])


def settle_kernel(flag_ref, *refs):
    moved = flag_ref[0] != 0
    for i in range(refs[-1].shape[0]):
        refs[-1][i] = jnp.where(moved, refs[2 * i + 1][...], refs[2 * i][...])


def settle(flag, arrays, ready):
    rows, feature = arrays[0].shape
    count = len(arrays) // 2
    steps = 2
    block = pl.BlockSpec((rows // steps, feature), lambda n: (n, 0))
    return pl.pallas_call(
        settle_kernel,
        grid=(steps,),
        out_shape=jax.ShapeDtypeStruct((count, rows, feature), BF16),
        in_specs=[pl.BlockSpec(memory_space=pltpu.SMEM)] + [block] * len(arrays)
        + [pl.BlockSpec(memory_space=pl.ANY)],
        out_specs=pl.BlockSpec((count, rows // steps, feature), lambda n: (0, n, 0)),
        compiler_params=pltpu.CompilerParams(vmem_limit_bytes=VMEM_LIMIT),
        cost_estimate=pl.CostEstimate(
            flops=count * rows * feature, bytes_accessed=6 * count * rows * feature, transcendentals=0
        ),
    )(flag, *arrays, ready)


def split_three(value):
    high = value.astype(BF16)
    rest = value - high.astype(F32)
    middle = rest.astype(BF16)
    low = (rest - middle.astype(F32)).astype(BF16)
    return high, middle, low


def body(tokens, cotangent, routes, route_weights, matching, gate_up, down, gate_up_m, gate_up_v,
         down_m, down_v):
    half = lax.axis_index("xh")
    rings = lax.axis_size("y") * lax.axis_size("z")
    ring = lax.axis_index("y") * lax.axis_size("z") + lax.axis_index("z")
    self_index = half * rings + ring
    swapped = jnp.sum(jnp.where(jnp.arange(2 * rings) == self_index, matching, 0)) != self_index
    flag = swapped.astype(jnp.int32).reshape(1)
    count, feature = tokens.shape
    slots = 2 * CAP

    top = routes.shape[1]
    named = jnp.concatenate([routes.astype(F32), route_weights], axis=1)
    named_other = swap(named, "xh")
    tokens_other = swap(tokens, "xh")
    cotangent_other = swap(cotangent, "xh")
    source = jnp.concatenate([tokens, cotangent, tokens_other, cotangent_other])

    w_own = jnp.concatenate([gate_up[0], down])
    w_first = after(w_own, tokens_other, cotangent_other, named_other)
    w_xl = swap(w_first, "xl")
    w_pair = swap(jnp.stack([w_own, w_xl]), "core")

    both = jnp.stack([named, named_other])
    both_routes = both[:, :, :top].astype(jnp.int32)
    both_weights = both[:, :, top:]
    ring_ids = jnp.arange(rings, dtype=jnp.int32)[:, None, None]
    hit = [both_routes[:, :, k] == half * rings + ring_ids for k in range(top)]
    used = sum(h.astype(jnp.int32) for h in hit)
    scale = sum(jnp.where(h, both_weights[:, :, k], 0.0) for k, h in enumerate(hit))
    before = (jnp.arange(count)[:, None] < jnp.arange(count)[None, :]).astype(BF16)
    earlier = jnp.dot(used.astype(BF16), before, preferred_element_type=F32).astype(jnp.int32)
    slot = earlier + CAP * jnp.arange(2, dtype=jnp.int32)[None, :, None]
    slot = jnp.where(used > 0, slot, -1)

    def on_lanes(value):
        return jnp.concatenate([value[:, 0], value[:, 0], value[:, 1], value[:, 1]], axis=1)[:, None]

    lane_kind = jnp.arange(4 * count, dtype=jnp.int32) // count % 2
    row = jnp.arange(2 * slots, dtype=jnp.int32)
    row = jnp.where(ring % 2 == 0, row, jnp.where(row < 8, row + 16, jnp.where(row < 16, row, row - 16)))
    row_kind = (row >= 12).astype(jnp.int32)
    row_slot = jnp.where(row < 12, row, jnp.where(row < 16, row - 4, row - 16))
    pick = (on_lanes(slot) == row_slot[:, None]) & (lane_kind == row_kind[:, None])
    lane_scale = jnp.where(lane_kind == 0, on_lanes(scale), 1.0)
    row_scale = jnp.sum(jnp.where(pick, on_lanes(scale), 0.0), axis=2)
    factor = jnp.where(row_kind == 0, 1.0, row_scale).reshape(-1, 1)
    pick_b = pick.astype(BF16).reshape(rings * 2 * slots, 4 * count)
    send = (dot_nn(pick_b, source) * factor).astype(BF16).reshape(rings, 2 * slots, feature)

    mv_xl = swap(after(jnp.concatenate([gate_up_m[0, :1], gate_up_v[0, :1]]), send), "xl")
    mv_up = swap(after(jnp.concatenate([gate_up_m[0, 1:], gate_up_v[0, 1:]]), send), "xl")

    recv = lax.all_to_all(send, RINGS, split_axis=0, concat_axis=0, tiled=True)
    back_send, xd, acts, *g_pair = rows_step(recv.reshape(-1, feature), w_own, w_xl, w_pair, mv_xl)

    g_core = [swap(g, "core") for g in g_pair]
    gate = grads_step(True, flag, xd, 0, acts, 0, g_core[0], mv_up)
    up = grads_step(True, flag, xd, 0, acts, 1, g_core[1], gate[0])
    down_g = grads_step(False, flag, xd, 1, acts, 2, g_core[2], up[0])
    back = lax.all_to_all(
        after(back_send, gate[0]).reshape(recv.shape), RINGS, split_axis=0, concat_axis=0, tiled=True
    ).reshape(-1, feature)
    parts = (gate[0], up[0], down_g[0], gate[1], up[1], down_g[1])
    others = [swap(parts[3], "xl"), swap(parts[4], "xl")]
    new_gate = adam_step(flag, (parts[0], ()), (others[0], ()), (gate_up, (0, 0)), (gate_up_m, (0, 0)),
                         (gate_up_v, (0, 0)), (w_xl, (0,)), (mv_xl, (0,)), (mv_xl, (1,)))
    others.append(swap(after(parts[5], new_gate), "xl"))
    gate_other = lax.ppermute(new_gate, ("xh", "xl"), ACROSS)
    new_up = adam_step(flag, (parts[1], ()), (others[1], ()), (gate_up, (0, 1)), (gate_up_m, (0, 1)),
                       (gate_up_v, (0, 1)), (w_xl, (1,)), (mv_up, (0,)), (mv_up, (1,)))
    arrived = [new_gate, gate_other, new_up, lax.ppermute(new_up, ("xh", "xl"), ACROSS)]
    new_gate_up = settle(flag, arrived, mv_xl)
    new_down = adam_step(flag, (parts[2], ()), (others[2], ()), (down, (0,)), (down_m, (0,)),
                         (down_v, (0,)))
    down_other = swap(new_down, "xh")

    mix = [
        jnp.where(pick, term, 0).reshape(rings * 2 * slots, 4 * count)
        for term in split_three(lane_scale)
    ]
    mixed = dot_tn(jnp.concatenate(mix, axis=1), back).reshape(3, 4 * count, feature)
    mixed = mixed[0] + mixed[1] + mixed[2]
    theirs = mixed[2 * count:].astype(BF16)
    ours = swap(theirs, "xh").astype(F32)
    layer_out = (mixed[:count] + ours[:count]).astype(BF16)
    input_grad = (mixed[count:2 * count] + ours[count:]).astype(BF16)
    new_down = settle(flag, [new_down, down_other], layer_out)
    return layer_out, input_grad, new_gate_up[None], new_down


def solution(mesh):
    wide = Mesh(mesh.devices.reshape(2, 4, 8, 2, 2), ALL)
    token_spec = P(ALL, None)
    expert, share = ("xh", "y", "z"), ("xl", "core")
    up_spec = P(expert, None, share, None)
    down_spec = P(expert, share, None)
    return jax.shard_map(
        body,
        mesh=wide,
        in_specs=(token_spec, token_spec, token_spec, token_spec, P(), up_spec, down_spec, up_spec,
                  up_spec, down_spec, down_spec),
        out_specs=(token_spec, token_spec, up_spec, down_spec),
        check_vma=False,
    )
```

```python
import functools

import jax
import jax.numpy as jnp
from jax import lax
from jax.experimental import pallas as pl
from jax.experimental.pallas import tpu as pltpu
from jax.sharding import Mesh, PartitionSpec as P

BETA_ONE = 0.9
BETA_TWO = 0.95
STEP_RATE = 0.01
ADAM_EPS = 1e-08

F32 = jnp.float32
BF16 = jnp.bfloat16
CAP = 6
RINGS = ("y", "z")
ACROSS = [(0, 3), (3, 0), (1, 2), (2, 1)]
ALL = ("xh", "y", "z", "xl", "core")


def swap(block, axis):
    return lax.ppermute(block, axis, [(0, 1), (1, 0)])


def after(value, *earlier):
    return lax.optimization_barrier((value, *earlier))[0]


def adam_update(weight, moment_one, moment_two, gradient):
    one_new = BETA_ONE * moment_one.astype(F32) + (1.0 - BETA_ONE) * gradient
    two_new = BETA_TWO * moment_two.astype(F32) + (1.0 - BETA_TWO) * gradient * gradient
    return (weight.astype(F32) - STEP_RATE * one_new / (jnp.sqrt(two_new) + ADAM_EPS)).astype(BF16)


def dot_nt(left, right):
    return lax.dot_general(left, right, (((1,), (1,)), ((), ())), preferred_element_type=F32)


def dot_nn(left, right):
    return lax.dot_general(left, right, (((1,), (0,)), ((), ())), preferred_element_type=F32)


def dot_tn(left, right):
    return lax.dot_general(left, right, (((0,), (0,)), ((), ())), preferred_element_type=F32)


CHUNK = 256
LANES = 1024
GROUP = 16
VMEM_LIMIT = 56 * 1024 * 1024


def mixed_order(size):
    to = lax.broadcasted_iota(jnp.int32, (size, size), 0)
    at = lax.broadcasted_iota(jnp.int32, (size, size), 1)
    part = to // (size // 2)
    row = to - part * (size // 2)
    return (at == (row // 4) * 8 + part * 4 + row % 4).astype(BF16)


def rows_kernel(rows_ref, w_own, w_xl, w_pair, _m, _v, back_ref, xd_out, act_out, g_gate, g_up, g_down,
                w_all, xd, mixed, acts, g_all, w_sem, xd_sem, act_sem, g_sem):
    share = w_own.shape[1]
    width = 4 * share
    rows = xd.shape[1]
    pairs = rows_ref.shape[0] // (3 * GROUP)
    plain = pairs * GROUP
    sources = (w_pair.at[0], w_pair.at[1], w_own, w_xl)
    loads = [
        pltpu.make_async_copy(src, w_all.at[:, pl.ds(i * share, share)], w_sem.at[i])
        for i, src in enumerate(sources)
    ]
    for load in loads:
        load.start()

    upper = lax.broadcasted_iota(jnp.int32, (GROUP, rows_ref.shape[1]), 0) < GROUP // 2

    def part(p, carry):
        base = pl.multiple_of(p * 3 * GROUP, GROUP)
        first = rows_ref[pl.ds(base, GROUP), :]
        last = rows_ref[pl.ds(base + 2 * GROUP, GROUP), :]
        to = pl.ds(pl.multiple_of(p * GROUP, GROUP), GROUP)
        xd[0, to, :] = jnp.where(upper, first, last)
        xd[1, to, :] = rows_ref[pl.ds(base + GROUP, GROUP), :]
        mixed[to, :] = jnp.where(upper, last, first)
        return carry

    lax.fori_loop(0, pairs, part, 0)
    order = mixed_order(plain)
    for n in range(0, rows_ref.shape[1], LANES):
        sorted_rows = dot_nn(order, mixed[:, n:n + LANES]).astype(BF16)
        xd[0, plain:, n:n + LANES] = sorted_rows[:plain // 2]
        xd[1, plain:, n:n + LANES] = sorted_rows[plain // 2:]
    xd_store = pltpu.make_async_copy(xd, xd_out, xd_sem)
    xd_store.start()

    done = 0
    for f in range(0, width, CHUNK):
        while done * share < f + CHUNK:
            loads[done].wait()
            done += 1
        a = dot_nt(xd[0], w_all[0, f:f + CHUNK, :])
        u = dot_nt(xd[0], w_all[1, f:f + CHUNK, :])
        s = 1.0 / (1.0 + jnp.exp(-a))
        dh = dot_nt(xd[1], w_all[2, f:f + CHUNK, :])
        acts[2, :, f:f + CHUNK] = (a * s * u).astype(BF16)
        acts[0, :, f:f + CHUNK] = (dh * u * s * (1.0 + a * (1.0 - s))).astype(BF16)
        acts[1, :, f:f + CHUNK] = (dh * a * s).astype(BF16)
    act_store = pltpu.make_async_copy(acts.at[:, :, pl.ds(2 * share, 2 * share)], act_out, act_sem)
    act_store.start()

    stores = []
    for i, (side, target) in enumerate(zip((0, 0, 1), (g_gate, g_up, g_down))):
        for n in range(0, rows_ref.shape[1], LANES):
            g_all[i, :, n:n + LANES] = dot_tn(
                acts[i, :, :2 * share], xd[side, :, n:n + LANES]
            ).astype(BF16)
        stores.append(pltpu.make_async_copy(g_all.at[i], target, g_sem.at[i]))
        stores[i].start()

    cut = lax.broadcasted_iota(jnp.int32, (GROUP, LANES), 0) < GROUP // 2
    for n in range(0, rows_ref.shape[1], LANES):
        o = dot_nn(acts[2], w_all[2, :, n:n + LANES]).astype(BF16)
        dx = (
            dot_nn(acts[0], w_all[0, :, n:n + LANES]) + dot_nn(acts[1], w_all[1, :, n:n + LANES])
        ).astype(BF16)
        blend = dot_tn(order, jnp.concatenate([o[plain:], dx[plain:]])).astype(BF16)
        for p in range(pairs):
            o_part = o[p * GROUP:(p + 1) * GROUP]
            m_part = blend[p * GROUP:(p + 1) * GROUP]
            base = p * 3 * GROUP
            back_ref[base:base + GROUP, n:n + LANES] = jnp.where(cut, o_part, m_part)
            back_ref[base + GROUP:base + 2 * GROUP, n:n + LANES] = dx[p * GROUP:(p + 1) * GROUP]
            back_ref[base + 2 * GROUP:base + 3 * GROUP, n:n + LANES] = jnp.where(cut, m_part, o_part)
    xd_store.wait()
    act_store.wait()
    for store in stores:
        store.wait()


def rows_step(rows, w_own, w_xl, w_pair, m_xl, v_xl):
    total, feature = rows.shape
    half = total // 2
    share = w_own.shape[1]
    any_spec = pl.BlockSpec(memory_space=pl.ANY)
    vmem_spec = pl.BlockSpec(memory_space=pltpu.VMEM)
    return pl.pallas_call(
        rows_kernel,
        out_shape=(
            jax.ShapeDtypeStruct(rows.shape, BF16),
            jax.ShapeDtypeStruct((2, half, feature), BF16),
            jax.ShapeDtypeStruct((3, half, 2 * share), BF16),
        ) + (jax.ShapeDtypeStruct((2 * share, feature), BF16),) * 3,
        in_specs=[vmem_spec] + [any_spec] * 5,
        out_specs=(vmem_spec,) + (any_spec,) * 5,
        scratch_shapes=[
            pltpu.VMEM((3, 4 * share, feature), BF16),
            pltpu.VMEM((2, half, feature), BF16),
            pltpu.VMEM((total // 3, feature), BF16),
            pltpu.VMEM((3, half, 4 * share), BF16),
            pltpu.VMEM((3, 2 * share, feature), BF16),
            pltpu.SemaphoreType.DMA((4,)),
            pltpu.SemaphoreType.DMA,
            pltpu.SemaphoreType.DMA,
            pltpu.SemaphoreType.DMA((3,)),
        ],
        compiler_params=pltpu.CompilerParams(vmem_limit_bytes=VMEM_LIMIT),
        cost_estimate=pl.CostEstimate(
            flops=half * feature * share,
            bytes_accessed=half * feature,
            transcendentals=0,
        ),
    )(rows, w_own, w_xl, w_pair, m_xl, v_xl)


def grads_kernel(exchange, flag_ref, rows_ref, act_ref, core_ref, *refs):
    keep_ref, send_ref = refs[-2:]
    share = core_ref.shape[0] // 2
    g = dot_tn(act_ref[...], rows_ref[...]) + core_ref[...].astype(F32)
    own, other = g[:share], g[share:]
    if exchange:
        moved = flag_ref[0] != 0
        own, other = jnp.where(moved, other, own), jnp.where(moved, own, other)
    keep_ref[...] = own.astype(BF16)
    send_ref[...] = other.astype(BF16)


def grads_step(exchange, flag, xd, side, acts, matrix, core, *ready):
    _, half, feature = xd.shape
    share = core.shape[0] // 2
    out = jax.ShapeDtypeStruct((share, feature), BF16)
    out_spec = pl.BlockSpec((share, LANES), lambda n: (0, n))
    return pl.pallas_call(
        functools.partial(grads_kernel, exchange),
        grid=(feature // LANES,),
        out_shape=(out,) * 2,
        in_specs=[
            pl.BlockSpec(memory_space=pltpu.SMEM),
            pl.BlockSpec((None, half, LANES), lambda n: (side, 0, n)),
            pl.BlockSpec((None, *acts.shape[1:]), lambda n: (matrix, 0, 0)),
            pl.BlockSpec((2 * share, LANES), lambda n: (0, n)),
        ] + [pl.BlockSpec(memory_space=pl.ANY)] * len(ready),
        out_specs=(out_spec,) * 2,
        compiler_params=pltpu.CompilerParams(vmem_limit_bytes=VMEM_LIMIT),
        cost_estimate=pl.CostEstimate(
            flops=4 * half * feature * share,
            bytes_accessed=2 * (half * feature + 4 * share * feature),
            transcendentals=0,
        ),
    )(flag, xd, acts, core, *ready)


def adam_kernel(flag_ref, keep_ref, recv_ref, *refs):
    moved = flag_ref[0] != 0
    out_ref = refs[-1]
    if len(refs) == 7:
        w, m, v = [
            jnp.where(moved, refs[i + 3][...].astype(F32), refs[i][...].astype(F32)) for i in range(3)
        ]
    else:
        w, m, v = [ref[...].astype(F32) for ref in refs[:3]]
    gradient = keep_ref[...].astype(F32) + recv_ref[...].astype(F32)
    out_ref[...] = adam_update(w, m, v, gradient)


def adam_step(flag, *arrays):
    rows, feature = arrays[0][0].shape[-2:]
    steps = 4

    def spec(lead):
        return pl.BlockSpec((None,) * len(lead) + (rows // steps, feature), lambda n: (*lead, n, 0))

    return pl.pallas_call(
        adam_kernel,
        grid=(steps,),
        out_shape=jax.ShapeDtypeStruct((rows, feature), BF16),
        in_specs=[pl.BlockSpec(memory_space=pltpu.SMEM)] + [spec(lead) for _, lead in arrays],
        out_specs=spec(()),
        compiler_params=pltpu.CompilerParams(vmem_limit_bytes=VMEM_LIMIT),
        cost_estimate=pl.CostEstimate(
            flops=20 * rows * feature,
            bytes_accessed=2 * (len(arrays) + 1) * rows * feature,
            transcendentals=rows * feature,
        ),
    )(flag, *[array for array, _ in arrays])


def settle_kernel(flag_ref, *refs):
    moved = flag_ref[0] != 0
    for i in range(refs[-1].shape[0]):
        refs[-1][i] = jnp.where(moved, refs[2 * i + 1][...], refs[2 * i][...])


def settle(flag, arrays, ready):
    rows, feature = arrays[0].shape
    count = len(arrays) // 2
    steps = 2
    block = pl.BlockSpec((rows // steps, feature), lambda n: (n, 0))
    return pl.pallas_call(
        settle_kernel,
        grid=(steps,),
        out_shape=jax.ShapeDtypeStruct((count, rows, feature), BF16),
        in_specs=[pl.BlockSpec(memory_space=pltpu.SMEM)] + [block] * len(arrays)
        + [pl.BlockSpec(memory_space=pl.ANY)],
        out_specs=pl.BlockSpec((count, rows // steps, feature), lambda n: (0, n, 0)),
        compiler_params=pltpu.CompilerParams(vmem_limit_bytes=VMEM_LIMIT),
        cost_estimate=pl.CostEstimate(
            flops=count * rows * feature, bytes_accessed=6 * count * rows * feature, transcendentals=0
        ),
    )(flag, *arrays, ready)


def split_three(value):
    high = value.astype(BF16)
    rest = value - high.astype(F32)
    middle = rest.astype(BF16)
    low = (rest - middle.astype(F32)).astype(BF16)
    return high, middle, low


def body(tokens, cotangent, routes, route_weights, matching, gate_up, down, gate_up_m, gate_up_v,
         down_m, down_v):
    half = lax.axis_index("xh")
    rings = lax.axis_size("y") * lax.axis_size("z")
    ring = lax.axis_index("y") * lax.axis_size("z") + lax.axis_index("z")
    self_index = half * rings + ring
    swapped = jnp.sum(jnp.where(jnp.arange(2 * rings) == self_index, matching, 0)) != self_index
    flag = swapped.astype(jnp.int32).reshape(1)
    count, feature = tokens.shape
    slots = 2 * CAP

    top = routes.shape[1]
    named = jnp.concatenate([routes.astype(F32), route_weights], axis=1)
    named_other = swap(named, "xh")
    tokens_other = swap(tokens, "xh")
    cotangent_other = swap(cotangent, "xh")
    source = jnp.concatenate([tokens, cotangent, tokens_other, cotangent_other])

    w_own = jnp.concatenate([gate_up[0], down])
    w_first = w_own
    w_xl = swap(w_first, "xl")

    both = jnp.stack([named, named_other])
    both_routes = both[:, :, :top].astype(jnp.int32)
    both_weights = both[:, :, top:]
    ring_ids = jnp.arange(rings, dtype=jnp.int32)[:, None, None]
    hit = [both_routes[:, :, k] == half * rings + ring_ids for k in range(top)]
    used = sum(h.astype(jnp.int32) for h in hit)
    scale = sum(jnp.where(h, both_weights[:, :, k], 0.0) for k, h in enumerate(hit))
    before = (jnp.arange(count)[:, None] < jnp.arange(count)[None, :]).astype(BF16)
    earlier = jnp.dot(used.astype(BF16), before, preferred_element_type=F32).astype(jnp.int32)
    slot = earlier + CAP * jnp.arange(2, dtype=jnp.int32)[None, :, None]
    slot = jnp.where(used > 0, slot, -1)

    def on_lanes(value):
        return jnp.concatenate([value[:, 0], value[:, 0], value[:, 1], value[:, 1]], axis=1)[:, None]

    lane_kind = jnp.arange(4 * count, dtype=jnp.int32) // count % 2
    row = jnp.arange(2 * slots, dtype=jnp.int32)
    row = jnp.where(ring % 2 == 0, row, jnp.where(row < 8, row + 16, jnp.where(row < 16, row, row - 16)))
    row_kind = (row >= 12).astype(jnp.int32)
    row_slot = jnp.where(row < 12, row, jnp.where(row < 16, row - 4, row - 16))
    pick = (on_lanes(slot) == row_slot[:, None]) & (lane_kind == row_kind[:, None])
    lane_scale = jnp.where(lane_kind == 0, on_lanes(scale), 1.0)
    row_scale = jnp.sum(jnp.where(pick, on_lanes(scale), 0.0), axis=2)
    factor = jnp.where(row_kind == 0, 1.0, row_scale).reshape(-1, 1)
    pick_b = pick.astype(BF16).reshape(rings * 2 * slots, 4 * count)
    send = (dot_nn(pick_b, source) * factor).astype(BF16).reshape(rings, 2 * slots, feature)

    m_xl = swap(after(gate_up_m[0, :1], send), "xl")
    v_xl = swap(after(gate_up_v[0, :1], send), "xl")
    w_pair = swap(jnp.stack([w_own, after(w_xl, m_xl)]), "core")

    recv = lax.all_to_all(send, RINGS, split_axis=0, concat_axis=0, tiled=True)
    back_send, xd, acts, *g_pair = rows_step(recv.reshape(-1, feature), w_own, w_xl, w_pair, m_xl, v_xl)

    g_core = [swap(g, "core") for g in g_pair]
    gate = grads_step(True, flag, xd, 0, acts, 0, g_core[0])
    up = grads_step(False, flag, xd, 0, acts, 1, g_core[1], gate[0])
    down_g = grads_step(False, flag, xd, 1, acts, 2, g_core[2], up[0])
    back = lax.all_to_all(
        after(back_send, gate[0]).reshape(recv.shape), RINGS, split_axis=0, concat_axis=0, tiled=True
    ).reshape(-1, feature)
    parts = (gate[0], up[0], down_g[0], gate[1], up[1], down_g[1])
    others = [swap(parts[3], "xl"), swap(parts[4], "xl")]
    new_gate = adam_step(flag, (parts[0], ()), (others[0], ()), (gate_up, (0, 0)), (gate_up_m, (0, 0)),
                         (gate_up_v, (0, 0)), (w_xl, (0,)), (m_xl, (0,)), (v_xl, (0,)))
    others.append(swap(after(parts[5], new_gate), "xl"))
    gate_other = lax.ppermute(new_gate, ("xh", "xl"), ACROSS)
    new_up = adam_step(flag, (parts[1], ()), (others[1], ()), (gate_up, (0, 1)), (gate_up_m, (0, 1)),
                       (gate_up_v, (0, 1)))
    arrived = [new_gate, gate_other, new_up, swap(new_up, "xh")]
    new_gate_up = settle(flag, arrived, m_xl)
    new_down = adam_step(flag, (parts[2], ()), (others[2], ()), (down, (0,)), (down_m, (0,)),
                         (down_v, (0,)))
    down_other = swap(new_down, "xh")

    mix = [
        jnp.where(pick, term, 0).reshape(rings * 2 * slots, 4 * count)
        for term in split_three(lane_scale)
    ]
    mixed = dot_tn(jnp.concatenate(mix, axis=1), back).reshape(3, 4 * count, feature)
    mixed = mixed[0] + mixed[1] + mixed[2]
    theirs = mixed[2 * count:].astype(BF16)
    ours = swap(theirs, "xh").astype(F32)
    layer_out = (mixed[:count] + ours[:count]).astype(BF16)
    input_grad = (mixed[count:2 * count] + ours[count:]).astype(BF16)
    new_down = settle(flag, [new_down, down_other], layer_out)
    return layer_out, input_grad, new_gate_up[None], new_down


def solution(mesh):
    wide = Mesh(mesh.devices.reshape(2, 4, 8, 2, 2), ALL)
    token_spec = P(ALL, None)
    expert, share = ("xh", "y", "z"), ("xl", "core")
    up_spec = P(expert, None, share, None)
    down_spec = P(expert, share, None)
    return jax.shard_map(
        body,
        mesh=wide,
        in_specs=(token_spec, token_spec, token_spec, token_spec, P(), up_spec, down_spec, up_spec,
                  up_spec, down_spec, down_spec),
        out_specs=(token_spec, token_spec, up_spec, down_spec),
        check_vma=False,
    )
```
